32 devices in a mesh: rows: 4 (over y, core), feat: 8 (over z, x).
Axes of the slice: x: 2, y: 2, z: 4, core: 2. Of those that a mesh axis runs over, the one named last changes fastest.
Arguments:
- samples: float32 [6144, 8192], P('rows', 'feat'), may hold values from -6 to 6
- whitening: float32 [8192, 1024], P('feat', 'rows'), may hold values from -0.09375 to 0.09375
- components: float32 [1024, 1024], P('rows', 'feat'), may hold values from -0.25 to 0.25
Outputs:
- moment: float32 [1024, 1024], P('rows', 'feat')
The draws below stay inside these ranges and needn't reach their ends.
All inputs are finite; a program needn't handle non-finite values.
Results may differ from the reference program's by a relative error of at most 0.00017.
Values sent between devices are 32-bit elements; how exact they have to be, the bound alone decides.
No kernel may reach another device: no remote copies, remote signals or barrier semaphores. Data moves between devices by JAX's collectives and lax.ppermute only.
A program may use at most 64 MiB of HBM per device.

```python
import jax
import jax.numpy as jnp
from jax import lax

F = 8192
K = 1024
R = 1024
ROWS = 6144


def strengthened(drawn, stream_key, source, target, blocks, factor):
    owner, partner = [(jnp.arange(drawn.shape[dim]) // (drawn.shape[dim] // blocks)).reshape([-1 if axis == dim else 1 for axis in range(drawn.ndim)]) for dim in (source, target)]
    chosen = jax.random.permutation(stream_key, blocks)[partner]
    strong = (owner == chosen) | (owner == (partner + blocks // 2) % blocks)
    return jnp.where(strong, factor * drawn, drawn)


def block_levels(own_key, shape, pieces, least, largest):
    def one(axis_at, blocks):
        heights = jax.random.uniform(jax.random.fold_in(jax.random.fold_in(own_key, 6), axis_at), (blocks,), jnp.float32, least / len(pieces), largest / len(pieces))
        return jnp.repeat(jnp.exp(heights), shape[axis_at] // blocks).reshape((-1,) + (1,) * (len(shape) - axis_at - 1))

    factor_of = one(*pieces[0])
    for cut in pieces[1:]:
        factor_of = factor_of * one(*cut)
    return factor_of


def bell_draw(key, extent, deviation, most, split=(), held_as=jnp.bfloat16):
    values = jax.random.normal(key, extent, jnp.float32) * deviation
    if len(split) > 0:
        values = block_levels(key, extent, split, -0.22, 0.18) * values
    return jnp.clip(values, min=-most, max=most).astype(held_as)


def heavy_noise(key, shape, deviation, limit, pieces, heavy, kind=jnp.bfloat16):
    array = deviation * jax.random.normal(key, shape, jnp.float32)
    if pieces:
        array = array * block_levels(key, shape, pieces, -0.22, 0.18)
    return jnp.clip(strengthened(array, jax.random.fold_in(key, 3), *heavy), -limit, limit).astype(kind)


def setup_inputs(seed: int = 0) -> dict:
    key_list = jax.random.split(jax.random.key(seed), 4)
    samples = bell_draw(key_list[0], (ROWS, F), 1.0, 6.0, ((0, 4), (1, 8)), jnp.float32)
    whitening = heavy_noise(key_list[1], (F, K), F ** -0.5, 0.09375, ((0, 8), (1, 4)), (0, 1, 8, 2.0), jnp.float32)
    components = heavy_noise(key_list[2], (K, R), K ** -0.5, 0.25, ((0, 4), (1, 8)), (0, 1, 8, 2.0), jnp.float32)
    return dict(samples=samples, whitening=whitening, components=components)


def reference(samples, whitening, components):
    whitened = jnp.dot(samples, whitening, precision=lax.Precision.HIGHEST, preferred_element_type=jnp.float32)
    projected = jnp.dot(whitened, components, precision=lax.Precision.HIGHEST, preferred_element_type=jnp.float32)
    squared = projected * projected
    total = lax.dot_general(whitened, squared, (((0,), (0,)), ((), ())), precision=lax.Precision.HIGHEST, preferred_element_type=jnp.float32)
    return total / jnp.sqrt(jnp.float32(ROWS))
```

```python
import functools

import jax
import jax.numpy as jnp
from jax import lax
from jax.experimental import pallas as pl
from jax.experimental.pallas import tpu as pltpu
from jax.sharding import PartitionSpec as P

VMEM_BYTES = 56 * 2**20


def cycle_of(mesh):
    line = list(mesh.devices[0])
    points = [tuple(d.coords) for d in line]
    moving = [a for a in range(len(points[0])) if len({p[a] for p in points}) > 1]
    if len(moving) != 2:
        return list(range(len(line)))
    inner = min(moving, key=lambda a: len({p[a] for p in points}))
    outer = moving[0] if inner == moving[1] else moving[1]
    at = {(p[outer], p[inner]): i for i, p in enumerate(points)}
    outers, inners = sorted({p[outer] for p in points}), sorted({p[inner] for p in points})
    walk = [at[o, inners[0]] for o in outers]
    for turn, o in enumerate(reversed(outers)):
        walk += [at[o, i] for i in (inners[1:] if turn % 2 == 0 else inners[:0:-1])]
    return walk


def split(a):
    high = a.astype(jnp.bfloat16)
    return high, (a - high.astype(jnp.float32)).astype(jnp.bfloat16)


def dot3(a, b, over=((1,), (0,))):
    def one(x, y):
        return lax.dot_general(x, y, (over, ((), ())), preferred_element_type=jnp.float32)

    return one(a[0], b[0]) + (one(a[0], b[1]) + one(a[1], b[0]))


def fill(high_ref, low_ref, refs):
    at = 0
    for ref in refs:
        width = ref.shape[1]
        high_ref[:, at : at + width], low_ref[:, at : at + width] = split(ref[...])
        at += width


def partial_kernel(samples_ref, *refs):
    *blocks, out_ref, high_ref, low_ref = refs

    @pl.when(pl.program_id(0) == 0)
    def _():
        fill(high_ref, low_ref, blocks)

    out_ref[...] = dot3(split(samples_ref[...]), (high_ref[...], low_ref[...]))


def partial_sums(samples, blocks, cost):
    rows, depth = samples.shape
    width = sum(b.shape[1] for b in blocks)
    tile = rows // 4 if rows % 32 == 0 else rows
    return pl.pallas_call(
        partial_kernel,
        out_shape=jax.ShapeDtypeStruct((rows, width), jnp.float32),
        grid=(rows // tile,),
        in_specs=[pl.BlockSpec((tile, depth), lambda i: (i, 0))]
        + [pl.BlockSpec(b.shape, lambda i: (0, 0)) for b in blocks],
        out_specs=pl.BlockSpec((tile, width), lambda i: (i, 0)),
        scratch_shapes=[pltpu.VMEM((depth, width), jnp.bfloat16)] * 2,
        compiler_params=pltpu.CompilerParams(vmem_limit_bytes=VMEM_BYTES),
        cost_estimate=pl.CostEstimate(
            flops=cost * 2 * rows * depth * width, bytes_accessed=4 * rows * (depth + width), transcendentals=0
        ),
    )(samples, *blocks)


def near_kernel(near_ref, *refs):
    *blocks, projected_ref, high_ref, low_ref, turned_high_ref, turned_low_ref = refs
    height = blocks[0].shape[0]
    near = split(near_ref[...])
    turned_high_ref[...], turned_low_ref[...] = near[0].T, near[1].T
    total = 0.0
    for k, block in enumerate(blocks):
        parts = split(block[...])
        if k < 2:
            mine = slice(k * height, (k + 1) * height)
            total = total + dot3((near[0][:, mine], near[1][:, mine]), parts)
        else:
            at = (k - 2) * height
            high_ref[at : at + height, :], low_ref[at : at + height, :] = parts
    projected_ref[...] = total


def near_terms(near, blocks):
    rows, depth = near.shape
    height, width = blocks[0].shape
    rest = height * (len(blocks) - 2)
    tile = width // 4 if width % 512 == 0 else width
    whole = lambda j: (0, 0)
    column = lambda j: (0, j)
    return pl.pallas_call(
        near_kernel,
        out_shape=[jax.ShapeDtypeStruct((rows, width), jnp.float32)]
        + [jax.ShapeDtypeStruct((rest, width), jnp.bfloat16)] * 2
        + [jax.ShapeDtypeStruct((depth, rows), jnp.bfloat16)] * 2,
        grid=(width // tile,),
        in_specs=[pl.BlockSpec(near.shape, whole)] + [pl.BlockSpec((height, tile), column) for _ in blocks],
        out_specs=[pl.BlockSpec((rows, tile), column)]
        + [pl.BlockSpec((rest, tile), column)] * 2
        + [pl.BlockSpec((depth, rows), whole)] * 2,
        compiler_params=pltpu.CompilerParams(vmem_limit_bytes=VMEM_BYTES),
        cost_estimate=pl.CostEstimate(
            flops=6 * rows * depth * width, bytes_accessed=12 * rest * width, transcendentals=0
        ),
    )(near, *blocks)


def moment_kernel(
    scale_inv, far_ref, projected_ref, comp_high_ref, comp_low_ref, near_high_ref, near_low_ref,
    kept_ref, sent_ref, high_ref, low_ref, turned_high_ref, turned_low_ref,
):
    @pl.when(pl.program_id(0) == 0)
    def _():
        high, low = split(far_ref[...])
        high_ref[...], low_ref[...] = high, low
        turned_high_ref[...], turned_low_ref[...] = high.T, low.T

    projected = projected_ref[...] + dot3(
        (high_ref[...], low_ref[...]), (comp_high_ref[...], comp_low_ref[...])
    )
    squared = split(projected * projected)
    pairs = ((near_high_ref, near_low_ref), (turned_high_ref, turned_low_ref))
    for out_ref, first in ((sent_ref, 1), (kept_ref, 0)):
        at = 0
        for high, low in pairs:
            width = high.shape[0] // 2
            mine = slice(first * width, (first + 1) * width)
            out_ref[at : at + width, :] = scale_inv * dot3((high[mine, :], low[mine, :]), squared)
            at += width


def moments(far, near_side, scale_inv):
    projected, comp_high, comp_low, near_high, near_low = near_side
    rows, width = projected.shape
    depth = near_high.shape[0] + far.shape[1]
    tile = width // 4 if width % 512 == 0 else width
    whole = lambda j: (0, 0)
    column = lambda j: (0, j)
    return pl.pallas_call(
        functools.partial(moment_kernel, scale_inv),
        out_shape=[jax.ShapeDtypeStruct((depth // 2, width), jnp.float32)] * 2,
        grid=(width // tile,),
        in_specs=[
            pl.BlockSpec(far.shape, whole),
            pl.BlockSpec((rows, tile), column),
            pl.BlockSpec((comp_high.shape[0], tile), column),
            pl.BlockSpec((comp_low.shape[0], tile), column),
            pl.BlockSpec(near_high.shape, whole),
            pl.BlockSpec(near_low.shape, whole),
        ],
        out_specs=[pl.BlockSpec((depth // 2, tile), column)] * 2,
        scratch_shapes=[pltpu.VMEM(far.shape, jnp.bfloat16)] * 2
        + [pltpu.VMEM(far.shape[::-1], jnp.bfloat16)] * 2,
        compiler_params=pltpu.CompilerParams(vmem_limit_bytes=VMEM_BYTES),
        cost_estimate=pl.CostEstimate(
            flops=12 * rows * depth * width, bytes_accessed=12 * depth * width, transcendentals=0
        ),
    )(far, *near_side)


def solution(mesh):
    n_rows, n_feat = mesh.shape["rows"], mesh.shape["feat"]
    cycle = cycle_of(mesh)
    place = [cycle.index(i) for i in range(n_feat)]
    onward = [(cycle[i], cycle[(i + 1) % n_feat]) for i in range(n_feat)]
    backward = [(b, a) for a, b in onward]
    high_bits = [1 << b for b in range(1, n_rows.bit_length() - 1)]

    def swap(a, bit):
        return lax.ppermute(a, "rows", [(i, i ^ bit) for i in range(n_rows)])

    def total_over_feat(a, dim):
        return lax.psum_scatter(
            a, "feat", scatter_dimension=dim, tiled=True, axis_index_groups=[cycle]
        )

    def ring_components(own, far):
        ahead, behind = [own], [own]
        for step in range(1, n_feat):
            if step == 3:
                far, ahead, behind = lax.optimization_barrier((far, ahead, behind))
            if step % 2:
                ahead.append(lax.ppermute(ahead[-1], "feat", onward))
            else:
                behind.append(lax.ppermute(behind[-1], "feat", backward))
        line = jnp.concatenate(ahead[::-1] + behind[1:], axis=1)
        first = (jnp.asarray(place)[lax.axis_index("feat")] - (len(ahead) - 1)) % n_feat
        return jnp.roll(line, first * own.shape[1], axis=1), far

    def over_high_bits(own):
        blocks = [own]
        for bit in high_bits:
            blocks += [swap(block, bit) for block in blocks]
        return blocks

    def on_device(samples, whitening, components):
        far = over_high_bits(whitening)[1:]
        near_part = partial_sums(samples, [whitening, swap(whitening, 1)], 40)
        near_sum = total_over_feat(near_part, 0)
        line, far = ring_components(components, far)
        far_part = partial_sums(samples, far + [swap(block, 1) for block in far], 15)
        far_sum = total_over_feat(far_part, 0)
        lines = over_high_bits(line)
        others = [swap(block, 1) for block in lines]
        blocks = [lines[0], others[0]] + lines[1:] + others[1:]
        scale_inv = float((samples.shape[0] * n_rows) ** -0.5)
        kept, sent = moments(far_sum, near_terms(near_sum, blocks), scale_inv)
        total = total_over_feat(kept + swap(sent, 1), 1)
        total = total.reshape(n_rows // 2, -1, total.shape[1])
        for bit in high_bits[::-1]:
            half = total.shape[0] // 2
            total = total[:half] + swap(total[half:], bit)
        return total[0]

    placed = (P("rows", "feat"), P("feat", "rows"), P("rows", "feat"))
    return jax.shard_map(
        on_device, mesh=mesh, in_specs=placed, out_specs=P("rows", "feat"), check_vma=False
    )
```

```python
import functools

import jax
import jax.numpy as jnp
import numpy as np
from jax import lax
from jax.experimental import pallas as pl
from jax.experimental.pallas import tpu as pltpu
from jax.sharding import PartitionSpec as P

VMEM_BYTES = 56 * 2**20
NEAR_COST, FAR_COST = 40, 0
EARLY, PINS = 2, 2
TIE1, TIE2 = 2, 3
ROWS_OVER_ROWS = ((0,), (0,))
LANES_OVER_LANES = ((1,), (1,))


def cycle_of(mesh):
    line = list(mesh.devices[0])
    points = [tuple(d.coords) for d in line]
    moving = [a for a in range(len(points[0])) if len({p[a] for p in points}) > 1]
    if len(moving) != 2:
        return list(range(len(line)))
    inner = min(moving, key=lambda a: len({p[a] for p in points}))
    outer = moving[0] if inner == moving[1] else moving[1]
    at = {(p[outer], p[inner]): i for i, p in enumerate(points)}
    outers, inners = sorted({p[outer] for p in points}), sorted({p[inner] for p in points})
    walk = [at[o, inners[0]] for o in outers]
    for turn, o in enumerate(reversed(outers)):
        walk += [at[o, i] for i in (inners[1:] if turn % 2 == 0 else inners[:0:-1])]
    return walk


def split(a):
    high = a.astype(jnp.bfloat16)
    return high, (a - high.astype(jnp.float32)).astype(jnp.bfloat16)


def dot3(a, b, over=((1,), (0,))):
    def one(x, y):
        return lax.dot_general(x, y, (over, ((), ())), preferred_element_type=jnp.float32)

    return one(a[0], b[0]) + (one(a[0], b[1]) + one(a[1], b[0]))


def call(kernel, out_shape, table, *args, grid=(), in_specs=None, out_specs=None, scratch_shapes=(), flops=0):
    whole = lambda a: pl.BlockSpec(a.shape, lambda *_: (0,) * len(a.shape))
    outs = list(out_shape)
    return pl.pallas_call(
        kernel,
        out_shape=outs,
        grid_spec=pltpu.PrefetchScalarGridSpec(
            num_scalar_prefetch=1,
            grid=grid or (1,),
            in_specs=in_specs or [whole(a) for a in args],
            out_specs=out_specs or [whole(a) for a in outs],
            scratch_shapes=list(scratch_shapes),
        ),
        compiler_params=pltpu.CompilerParams(vmem_limit_bytes=VMEM_BYTES),
        cost_estimate=pl.CostEstimate(flops=flops, bytes_accessed=sum(4 * a.size for a in args), transcendentals=0),
    )(table, *args)


def f32(*shape):
    return jax.ShapeDtypeStruct(shape, jnp.float32)


def bf16(*shape):
    return jax.ShapeDtypeStruct(shape, jnp.bfloat16)


def partial_kernel(core_at, n_tiles, table, *refs):
    tiles, blocks, (out_ref, high_ref, low_ref) = refs[:n_tiles], refs[n_tiles:-3], refs[-3:]
    width = blocks[0].shape[1]
    for core in (0, 1):

        @pl.when((pl.program_id(0) == 0) & (table[core_at] == core))
        def _():
            for k, ref in enumerate(blocks):
                at = (k // 2 * 2 + (k % 2 ^ core)) * width
                high_ref[:, at : at + width], low_ref[:, at : at + width] = split(ref[...])

    rows = jnp.concatenate([ref[...] for ref in tiles], axis=0)
    out_ref[...] = dot3(split(rows), (high_ref[...], low_ref[...]))


def partial_sums(samples, blocks, table, pieces, core_at, cost):
    rows, depth = samples.shape
    width = sum(b.shape[1] for b in blocks)
    height = rows // pieces
    together = max(k for k in (1, 2, 4) if pieces % k == 0 and (k == 1 or height * k <= 384))

    def part(first, steps):
        return call(
            functools.partial(partial_kernel, core_at, together),
            [f32(height * together * steps, width)],
            table,
            *[samples] * together,
            *blocks,
            grid=(steps,),
            in_specs=[
                pl.BlockSpec((height, depth), lambda i, t, k=k: (t[(i + first) * together + k], 0))
                for k in range(together)
            ]
            + [pl.BlockSpec(b.shape, lambda i, t: (0, 0)) for b in blocks],
            out_specs=[pl.BlockSpec((height * together, width), lambda i, t: (i, 0))],
            scratch_shapes=[pltpu.VMEM((depth, width), jnp.bfloat16)] * 2,
            flops=cost * 2 * height * together * steps * depth * width,
        )[0]

    return part(0, 1), part(1, pieces // together - 1)


def near_kernel(order_at, table, *refs):
    *pieces, near_ref, far_ref, projected_ref, high_ref, low_ref, near_high_ref, near_low_ref = refs
    height = pieces[0].shape[0]
    for k, ref in enumerate(pieces):
        rows = slice(k * height, (k + 1) * height)
        near_high_ref[rows, :], near_low_ref[rows, :] = split(ref[...])
    n, height, _ = near_ref.shape
    near = []
    for k in range(n):
        at = table[order_at + k]
        near.append(near_ref[at])
        rows = slice(k * height, (k + 1) * height)
        high_ref[rows, :], low_ref[rows, :] = split(far_ref[at])
    near = split(jnp.concatenate(near, axis=0))
    projected_ref[...] = dot3(near, (near_high_ref[...], near_low_ref[...]), LANES_OVER_LANES)


def moment_kernel(scale_inv, n_high, table, *refs):
    projected_ref, comp_high_ref, comp_low_ref, near_high_ref, near_low_ref, *refs = refs
    *pieces, out0_ref, out1_ref, high_ref, low_ref = refs

    @pl.when(pl.program_id(0) == 0)
    def _():
        height = pieces[0].shape[0]
        for k, ref in enumerate(pieces):
            rows = slice(k * height, (k + 1) * height)
            high_ref[rows, :], low_ref[rows, :] = split(ref[...])

    projected = projected_ref[...] + dot3(
        (comp_high_ref[...], comp_low_ref[...]), (high_ref[...], low_ref[...]), LANES_OVER_LANES
    )
    squared = split(projected * projected)
    near = dot3(squared, (near_high_ref[...], near_low_ref[...])) * scale_inv
    far = dot3(squared, (high_ref[...], low_ref[...])) * scale_inv
    width = near.shape[1] // 2
    for core, ref in enumerate((out0_ref, out1_ref)):
        ref[:, :width] = near[:, core * width : (core + 1) * width]
        for h in range(1, n_high):
            at = (2 * (h - 1) + core) * width
            ref[:, h * width : (h + 1) * width] = far[:, at : at + width]


def divide_kernel(core_at, table, own_ref, *refs):
    *others, kept_ref, sent_ref = refs
    total = own_ref[...]
    for ref in others:
        total = total + ref[...]
    width = kept_ref.shape[1]
    for core in (0, 1):

        @pl.when(table[core_at] == core)
        def _():
            kept_ref[...] = total[:, core * width : (core + 1) * width]
            sent_ref[...] = total[:, (1 - core) * width : (2 - core) * width]


def assemble_kernel(core_at, table, own_ref, other_ref, out_ref):
    for core in (0, 1):

        @pl.when(table[core_at] == core)
        def _():
            pair = (own_ref[...], other_ref[...])
            out_ref[...] = jnp.concatenate(pair[:: 1 - 2 * core], axis=0).T


def solution(mesh):
    n_rows, n_feat = mesh.shape["rows"], mesh.shape["feat"]
    cycle = cycle_of(mesh)
    place = [cycle.index(i) for i in range(n_feat)]
    n_high = n_rows // 2
    high_bits = [1 << b for b in range(1, n_rows.bit_length() - 1)]
    both = ("rows", "feat")
    streams = [
        [
            (r * n_feat + cycle[i], r * n_feat + cycle[(i + (1 if r % 2 == s else -1)) % n_feat])
            for r in range(n_rows)
            for i in range(n_feat)
        ]
        for s in (0, 1)
    ]
    order = [j for j in range(n_feat) if j % 2 == 0] + [j for j in range(n_feat) if j % 2]
    pieces, reach = n_feat, n_feat // 2
    core_at, order_at = pieces, pieces + 1
    cut = max(1, reach // 2)
    held_order = [0, *range(1, cut + 1), *(n_feat - k for k in range(1, min(cut, reach - 1) + 1))]
    held_order += [*range(cut + 1, reach + 1), *(n_feat - k for k in range(cut + 1, reach))]
    facts = np.zeros((2, n_feat, order_at + n_feat), np.int32)
    for core in (0, 1):
        for f in range(n_feat):
            p, way = place[f], 1 - 2 * core
            for t in range(reach):
                facts[core, f, 2 * t] = (p + way * (reach - t)) % n_feat
                facts[core, f, 2 * t + 1] = (p - way * (reach - 1 - t)) % n_feat
            facts[core, f, core_at] = core
            for k, j in enumerate(order):
                away = way * (p - place[f ^ j]) % n_feat
                facts[core, f, order_at + k] = held_order.index(away)

    def swap(a, bit):
        return lax.ppermute(a, "rows", [(i, i ^ bit) for i in range(n_rows)])

    def swap_feat(a, bit):
        return lax.ppermute(a, "feat", [(i, i ^ bit) for i in range(n_feat)])

    def over_high_bits(own):
        blocks = [own]
        for bit in high_bits:
            blocks += [swap(block, bit) for block in blocks]
        return blocks

    def on_device(samples, whitening, components):
        core = lax.axis_index("rows") % 2
        table = lax.dynamic_slice(
            jnp.asarray(facts), (core, lax.axis_index("feat"), 0), (1, 1, facts.shape[2])
        ).reshape(-1)
        height = samples.shape[0] // pieces

        def rounds(part, first, last, held):
            for t in range(first, last):
                for s in (0, 1):
                    at = 2 * t + s
                    cut_at = part[0].shape[0] // height
                    source, at_row = (part[0], at) if at < cut_at else (part[1], at - cut_at)
                    piece = source[at_row * height : (at_row + 1) * height]
                    if t == 0:
                        held[s] = piece
                    elif at < n_feat:
                        held[s] = lax.ppermute(held[s], both, streams[s]) + piece
            return held

        far = over_high_bits(whitening)[1:]
        near_part = partial_sums(samples, [whitening, swap(whitening, 1)], table, pieces, core_at, NEAR_COST)

        turned = components.T
        turned = turned.reshape(2, turned.shape[0] // 2, -1)
        mine, others = (
            lax.dynamic_index_in_dim(turned, c, keepdims=False) for c in (core, 1 - core)
        )
        others = swap(others, 1)
        first = core == 0
        own = jnp.concatenate([jnp.where(first, mine, others), jnp.where(first, others, mine)], axis=1)
        line, groups = {0: own}, []

        def pass_components(first, last):
            for step in range(first, last):
                line[step] = lax.ppermute(line[step - 1], both, streams[0])
                if step < reach:
                    line[n_feat - step] = lax.ppermute(line[(n_feat - step + 1) % n_feat], both, streams[1])
                if step in (cut, reach):
                    done = sum(g.shape[0] for g in groups)
                    groups.append(jnp.stack([line[away] for away in held_order[done : len(line)]]))

        pass_components(1, 2)
        first_near, line = lax.optimization_barrier((near_part[0], line))
        near_part = (first_near, near_part[1])
        near = rounds(near_part, 0, 1, [None, None])
        for t in range(1, reach):
            if t == EARLY:
                far, near = lax.optimization_barrier((far, near))
                far_blocks = []
                for block in far:
                    far_blocks += [block, swap(block, 1)]
                far_part = partial_sums(samples, far_blocks, table, pieces, core_at, FAR_COST)
            if t < PINS:
                pass_components(t + 1, t + 2)
            near = rounds(near_part, t, t + 1, near)
            if t < PINS:
                near, line = lax.optimization_barrier((near, line))
            if t == EARLY:
                first_far, line = lax.optimization_barrier((far_part[0], line))
                far_part = (first_far, far_part[1])
        near = lax.ppermute(near[0], both, streams[0]) + near[1]
        pass_components(min(PINS + 1, reach + 1), reach + 1)

        held = rounds(far_part, 0, min(TIE1, reach), [None, None])
        over = over_high_bits(groups[0])
        held, over = lax.optimization_barrier((held, over))
        held = rounds(far_part, min(TIE1, reach), min(TIE2, reach), held)
        over = [over] + [over_high_bits(g) for g in groups[1:]]
        held, over = lax.optimization_barrier((held, over))
        near_stack, *far_stacks = [jnp.concatenate(parts) for parts in zip(*over)]
        far_stack = jnp.concatenate(far_stacks, axis=2) if n_high > 2 else far_stacks[0]
        near_rows = [near, swap(near, 1)]
        n_wide, n_tall = near_stack.shape[2], n_feat * near_stack.shape[1]
        f_wide, n_deep = far_stack.shape[2], 2 * height
        near_side = call(
            functools.partial(near_kernel, order_at),
            [f32(n_tall, n_deep), bf16(n_tall, f_wide), bf16(n_tall, f_wide), bf16(n_deep, n_wide), bf16(n_deep, n_wide)],
            table,
            *near_rows,
            near_stack,
            far_stack,
            flops=6 * n_tall * n_deep * n_wide,
        )
        held = rounds(far_part, min(TIE2, reach), reach, held)
        arrived = lax.ppermute(held[0], both, streams[0])
        arrived, near_side = lax.optimization_barrier((arrived, near_side))
        far_sum = arrived + held[1]
        far_rows = [far_sum, swap(far_sum, 1)]
        scale_inv = float((samples.shape[0] * n_rows) ** -0.5)
        tile = n_tall // 2
        whole = lambda a: pl.BlockSpec(a.shape, lambda i, t: (0, 0))
        tiled = lambda a: pl.BlockSpec((tile, a.shape[1]), lambda i, t: (i, 0))
        half_wide = n_high * (n_wide // 2)
        a, b = call(
            functools.partial(moment_kernel, scale_inv, n_high),
            [f32(n_tall, half_wide)] * 2,
            table,
            *near_side,
            *far_rows,
            grid=(n_tall // tile,),
            in_specs=[tiled(x) for x in near_side[:3]] + [whole(x) for x in near_side[3:]] + [whole(x) for x in far_rows],
            out_specs=[pl.BlockSpec((tile, half_wide), lambda i, t: (i, 0))] * 2,
            scratch_shapes=[pltpu.VMEM((n_deep, f_wide), jnp.bfloat16)] * 2,
            flops=6 * n_tall * n_deep * (n_wide + 2 * f_wide),
        )

        def over_rows(x):
            for bit in high_bits[::-1]:
                half = x.shape[1] // 2
                x = x[:, :half] + swap(x[:, half:], bit)
            return x

        def over_first_bit(x):
            half = x.shape[0] // 2
            return x[:half] + swap_feat(x[half:], 1)

        a, b = over_first_bit(over_rows(a)), over_rows(over_first_bit(b))
        joint = jnp.concatenate([a, b], axis=1)
        step = joint.shape[0] // (n_feat // 2)
        parts = [joint[k * step : (k + 1) * step] for k in range(n_feat // 2)]
        parts = parts[:1] + [swap_feat(part, 2 * k) for k, part in enumerate(parts) if k]
        width = joint.shape[1] // 2
        kept, sent = call(
            functools.partial(divide_kernel, core_at), [f32(step, width)] * 2, table, *parts
        )
        return call(
            functools.partial(assemble_kernel, core_at), [f32(width, 2 * step)], table, kept, swap(sent, 1)
        )[0]

    placed = (P("rows", "feat"), P("feat", "rows"), P("rows", "feat"))
    return jax.shard_map(
        on_device, mesh=mesh, in_specs=placed, out_specs=P("rows", "feat"), check_vma=False
    )
```

```python
import functools

import jax
import jax.numpy as jnp
import numpy as np
from jax import lax
from jax.experimental import pallas as pl
from jax.experimental.pallas import tpu as pltpu
from jax.sharding import PartitionSpec as P

VMEM_BYTES = 40 * 2**20
NEAR_COST, FAR_COST = 40, 0
EARLY, PINS = 2, 2
TIE1, TIE2 = 2, 3
ROWS_OVER_ROWS = ((0,), (0,))
LANES_OVER_LANES = ((1,), (1,))


def cycle_of(mesh):
    line = list(mesh.devices[0])
    points = [tuple(d.coords) for d in line]
    moving = [a for a in range(len(points[0])) if len({p[a] for p in points}) > 1]
    if len(moving) != 2:
        return list(range(len(line)))
    inner = min(moving, key=lambda a: len({p[a] for p in points}))
    outer = moving[0] if inner == moving[1] else moving[1]
    at = {(p[outer], p[inner]): i for i, p in enumerate(points)}
    outers, inners = sorted({p[outer] for p in points}), sorted({p[inner] for p in points})
    walk = [at[o, inners[0]] for o in outers]
    for turn, o in enumerate(reversed(outers)):
        walk += [at[o, i] for i in (inners[1:] if turn % 2 == 0 else inners[:0:-1])]
    return walk


def split(a):
    high = a.astype(jnp.bfloat16)
    return high, (a - high.astype(jnp.float32)).astype(jnp.bfloat16)


def dot3(a, b, over=((1,), (0,))):
    def one(x, y):
        return lax.dot_general(x, y, (over, ((), ())), preferred_element_type=jnp.float32)

    return one(a[0], b[0]) + (one(a[0], b[1]) + one(a[1], b[0]))


def call(kernel, out_shape, table, *args, grid=(), in_specs=None, out_specs=None, scratch_shapes=(), flops=0, grant=VMEM_BYTES):
    whole = lambda a: pl.BlockSpec(a.shape, lambda *_: (0,) * len(a.shape))
    outs = list(out_shape)
    return pl.pallas_call(
        kernel,
        out_shape=outs,
        grid_spec=pltpu.PrefetchScalarGridSpec(
            num_scalar_prefetch=1,
            grid=grid or (1,),
            in_specs=in_specs or [whole(a) for a in args],
            out_specs=out_specs or [whole(a) for a in outs],
            scratch_shapes=list(scratch_shapes),
        ),
        compiler_params=pltpu.CompilerParams(vmem_limit_bytes=grant),
        cost_estimate=pl.CostEstimate(flops=flops, bytes_accessed=sum(4 * a.size for a in args), transcendentals=0),
    )(table, *args)


def f32(*shape):
    return jax.ShapeDtypeStruct(shape, jnp.float32)


def bf16(*shape):
    return jax.ShapeDtypeStruct(shape, jnp.bfloat16)


def partial_kernel(core_at, n_tiles, table, *refs):
    tiles, blocks, (out_ref, high_ref, low_ref) = refs[:n_tiles], refs[n_tiles:-3], refs[-3:]
    width = blocks[0].shape[1]
    for core in (0, 1):

        @pl.when((pl.program_id(0) == 0) & (table[core_at] == core))
        def _():
            for k, ref in enumerate(blocks):
                at = (k // 2 * 2 + (k % 2 ^ core)) * width
                high_ref[:, at : at + width], low_ref[:, at : at + width] = split(ref[...])

    rows = jnp.concatenate([ref[...] for ref in tiles], axis=0)
    out_ref[...] = dot3(split(rows), (high_ref[...], low_ref[...]))


def partial_sums(samples, blocks, table, pieces, core_at, cost):
    rows, depth = samples.shape
    width = sum(b.shape[1] for b in blocks)
    height = rows // pieces
    together = max(k for k in (1, 2, 4) if pieces % k == 0 and (k == 1 or height * k <= 384))

    def part(first, steps):
        return call(
            functools.partial(partial_kernel, core_at, together),
            [f32(height * together * steps, width)],
            table,
            *[samples] * together,
            *blocks,
            grid=(steps,),
            in_specs=[
                pl.BlockSpec((height, depth), lambda i, t, k=k: (t[(i + first) * together + k], 0))
                for k in range(together)
            ]
            + [pl.BlockSpec(b.shape, lambda i, t: (0, 0)) for b in blocks],
            out_specs=[pl.BlockSpec((height * together, width), lambda i, t: (i, 0))],
            scratch_shapes=[pltpu.VMEM((depth, width), jnp.bfloat16)] * 2,
            flops=cost * 2 * height * together * steps * depth * width,
        )[0]

    return part(0, 1), part(1, pieces // together - 1)


def near_kernel(order_at, table, *refs):
    *pieces, near_ref, far_ref, projected_ref, high_ref, low_ref, near_high_ref, near_low_ref = refs
    height = pieces[0].shape[0]
    for k, ref in enumerate(pieces):
        rows = slice(k * height, (k + 1) * height)
        near_high_ref[rows, :], near_low_ref[rows, :] = split(ref[...])
    n, height, _ = near_ref.shape
    near = []
    for k in range(n):
        at = table[order_at + k]
        near.append(near_ref[at])
        rows = slice(k * height, (k + 1) * height)
        high_ref[rows, :], low_ref[rows, :] = split(far_ref[at])
    near = split(jnp.concatenate(near, axis=0))
    projected_ref[...] = dot3(near, (near_high_ref[...], near_low_ref[...]), LANES_OVER_LANES)


def columns_of(near, far, width, core, highs):
    parts = []
    for h in highs:
        at = core * width if h == 0 else (2 * (h - 1) + core) * width
        parts.append((near if h == 0 else far)[:, at : at + width])
    return parts


def store_moments(ref, squared, scale_inv, columns):
    at = 0
    for high, low in columns:
        width = high.shape[1]
        ref[:, at : at + width] = scale_inv * dot3(squared, (high, low))
        at += width


def sent_kernel(scale_inv, n_high, table, *refs):
    projected_ref, comp_high_ref, comp_low_ref, near_high_ref, near_low_ref, *refs = refs
    *pieces, a_ref, b_ref, sq_high_ref, sq_low_ref, far_high_ref, far_low_ref = refs

    @pl.when(pl.program_id(0) == 0)
    def _():
        height = pieces[0].shape[0]
        for k, ref in enumerate(pieces):
            rows = slice(k * height, (k + 1) * height)
            far_high_ref[rows, :], far_low_ref[rows, :] = split(ref[...])

    projected = projected_ref[...] + dot3(
        (comp_high_ref[...], comp_low_ref[...]), (far_high_ref[...], far_low_ref[...]), LANES_OVER_LANES
    )
    squared = split(projected * projected)
    sq_high_ref[...], sq_low_ref[...] = squared
    width = near_high_ref.shape[1] // 2

    def columns(core, highs):
        return zip(
            columns_of(near_high_ref, far_high_ref, width, core, highs),
            columns_of(near_low_ref, far_low_ref, width, core, highs),
        )

    store_moments(a_ref, squared, scale_inv, columns(0, range(n_high // 2, n_high)))

    @pl.when(pl.program_id(0) == 1)
    def _():
        store_moments(b_ref, squared, scale_inv, columns(1, range(n_high)))


def kept_kernel(scale_inv, n_high, table, *refs):
    sq_high_ref, sq_low_ref, near_high_ref, near_low_ref, far_high_ref, far_low_ref, a_ref, b_ref = refs
    squared = sq_high_ref[...], sq_low_ref[...]
    width = near_high_ref.shape[1] // 2

    def columns(core, highs):
        return zip(
            columns_of(near_high_ref, far_high_ref, width, core, highs),
            columns_of(near_low_ref, far_low_ref, width, core, highs),
        )

    store_moments(a_ref, squared, scale_inv, columns(0, range(n_high // 2)))

    @pl.when(pl.program_id(0) == 0)
    def _():
        store_moments(b_ref, squared, scale_inv, columns(1, range(n_high)))


def divide_kernel(core_at, table, own_ref, *refs):
    *others, kept_ref, sent_ref = refs
    total = own_ref[...]
    for ref in others:
        total = total + ref[...]
    width = kept_ref.shape[1]
    for core in (0, 1):

        @pl.when(table[core_at] == core)
        def _():
            kept_ref[...] = total[:, core * width : (core + 1) * width]
            sent_ref[...] = total[:, (1 - core) * width : (2 - core) * width]


def assemble_kernel(core_at, table, own_ref, other_ref, out_ref):
    for core in (0, 1):

        @pl.when(table[core_at] == core)
        def _():
            pair = (own_ref[...], other_ref[...])
            out_ref[...] = jnp.concatenate(pair[:: 1 - 2 * core], axis=0).T


def solution(mesh):
    n_rows, n_feat = mesh.shape["rows"], mesh.shape["feat"]
    cycle = cycle_of(mesh)
    place = [cycle.index(i) for i in range(n_feat)]
    n_high = n_rows // 2
    high_bits = [1 << b for b in range(1, n_rows.bit_length() - 1)]
    both = ("rows", "feat")
    streams = [
        [
            (r * n_feat + cycle[i], r * n_feat + cycle[(i + (1 if r % 2 == s else -1)) % n_feat])
            for r in range(n_rows)
            for i in range(n_feat)
        ]
        for s in (0, 1)
    ]
    order = [j for j in range(n_feat) if j % 2 == 0] + [j for j in range(n_feat) if j % 2]
    pieces, reach = n_feat, n_feat // 2
    core_at, order_at = pieces, pieces + 1
    cut = max(1, reach // 2)
    held_order = [0, *range(1, cut + 1), *(n_feat - k for k in range(1, min(cut, reach - 1) + 1))]
    held_order += [*range(cut + 1, reach + 1), *(n_feat - k for k in range(cut + 1, reach))]
    facts = np.zeros((2, n_feat, order_at + n_feat), np.int32)
    for core in (0, 1):
        for f in range(n_feat):
            p, way = place[f], 1 - 2 * core
            for t in range(reach):
                facts[core, f, 2 * t] = (p + way * (reach - t)) % n_feat
                facts[core, f, 2 * t + 1] = (p - way * (reach - 1 - t)) % n_feat
            facts[core, f, core_at] = core
            for k, j in enumerate(order):
                away = way * (p - place[f ^ j]) % n_feat
                facts[core, f, order_at + k] = held_order.index(away)

    def swap(a, bit):
        return lax.ppermute(a, "rows", [(i, i ^ bit) for i in range(n_rows)])

    def swap_feat(a, bit):
        return lax.ppermute(a, "feat", [(i, i ^ bit) for i in range(n_feat)])

    def over_high_bits(own):
        blocks = [own]
        for bit in high_bits:
            blocks += [swap(block, bit) for block in blocks]
        return blocks

    def on_device(samples, whitening, components):
        core = lax.axis_index("rows") % 2
        table = lax.dynamic_slice(
            jnp.asarray(facts), (core, lax.axis_index("feat"), 0), (1, 1, facts.shape[2])
        ).reshape(-1)
        height = samples.shape[0] // pieces

        def rounds(part, first, last, held):
            for t in range(first, last):
                for s in (0, 1):
                    at = 2 * t + s
                    cut_at = part[0].shape[0] // height
                    source, at_row = (part[0], at) if at < cut_at else (part[1], at - cut_at)
                    piece = source[at_row * height : (at_row + 1) * height]
                    if t == 0:
                        held[s] = piece
                    elif at < n_feat:
                        held[s] = lax.ppermute(held[s], both, streams[s]) + piece
            return held

        far = over_high_bits(whitening)[1:]
        near_part = partial_sums(samples, [whitening, swap(whitening, 1)], table, pieces, core_at, NEAR_COST)

        turned = components.T
        turned = turned.reshape(2, turned.shape[0] // 2, -1)
        mine, others = (
            lax.dynamic_index_in_dim(turned, c, keepdims=False) for c in (core, 1 - core)
        )
        others = swap(others, 1)
        first = core == 0
        own = jnp.concatenate([jnp.where(first, mine, others), jnp.where(first, others, mine)], axis=1)
        line, groups = {0: own}, []

        def pass_components(first, last):
            for step in range(first, last):
                line[step] = lax.ppermute(line[step - 1], both, streams[0])
                if step < reach:
                    line[n_feat - step] = lax.ppermute(line[(n_feat - step + 1) % n_feat], both, streams[1])
                if step in (cut, reach):
                    done = sum(g.shape[0] for g in groups)
                    groups.append(jnp.stack([line[away] for away in held_order[done : len(line)]]))

        pass_components(1, 2)
        first_near, line = lax.optimization_barrier((near_part[0], line))
        near_part = (first_near, near_part[1])
        near = rounds(near_part, 0, 1, [None, None])
        for t in range(1, reach):
            if t == EARLY:
                far, near = lax.optimization_barrier((far, near))
                far_blocks = []
                for block in far:
                    far_blocks += [block, swap(block, 1)]
                far_part = partial_sums(samples, far_blocks, table, pieces, core_at, FAR_COST)
            if t < PINS:
                pass_components(t + 1, t + 2)
            near = rounds(near_part, t, t + 1, near)
            if t < PINS:
                near, line = lax.optimization_barrier((near, line))
            if t == EARLY:
                first_far, line = lax.optimization_barrier((far_part[0], line))
                far_part = (first_far, far_part[1])
        near = lax.ppermute(near[0], both, streams[0]) + near[1]
        pass_components(min(PINS + 1, reach + 1), reach + 1)

        held = rounds(far_part, 0, min(TIE1, reach), [None, None])
        over = over_high_bits(groups[0])
        held, over = lax.optimization_barrier((held, over))
        held = rounds(far_part, min(TIE1, reach), min(TIE2, reach), held)
        over = [over] + [over_high_bits(g) for g in groups[1:]]
        held, over = lax.optimization_barrier((held, over))
        near_stack, *far_stacks = [jnp.concatenate(parts) for parts in zip(*over)]
        far_stack = jnp.concatenate(far_stacks, axis=2) if n_high > 2 else far_stacks[0]
        near_rows = [near, swap(near, 1)]
        n_wide, n_tall = near_stack.shape[2], n_feat * near_stack.shape[1]
        f_wide, n_deep = far_stack.shape[2], 2 * height
        near_side = call(
            functools.partial(near_kernel, order_at),
            [f32(n_tall, n_deep), bf16(n_tall, f_wide), bf16(n_tall, f_wide), bf16(n_deep, n_wide), bf16(n_deep, n_wide)],
            table,
            *near_rows,
            near_stack,
            far_stack,
            flops=6 * n_tall * n_deep * n_wide,
        )
        held = rounds(far_part, min(TIE2, reach), reach, held)
        arrived = lax.ppermute(held[0], both, streams[0])
        arrived, near_side = lax.optimization_barrier((arrived, near_side))
        far_sum = arrived + held[1]
        far_rows = [far_sum, swap(far_sum, 1)]
        scale_inv = float((samples.shape[0] * n_rows) ** -0.5)
        tile, wide = n_tall // 2, n_wide // 2
        whole = lambda a: pl.BlockSpec(a.shape, lambda i, t: (0, 0))
        tiled = lambda a: pl.BlockSpec((tile, a.shape[1]), lambda i, t: (i, 0))
        half_a, half_b = f32(n_tall, n_high // 2 * wide), f32(tile, n_high * wide)
        squares, rows_split = [bf16(n_tall, n_deep)] * 2, [bf16(n_deep, f_wide)] * 2
        a_sent, b_sent, *squared_and_far = call(
            functools.partial(sent_kernel, scale_inv, n_high),
            [half_a, half_b] + squares + rows_split,
            table,
            *near_side,
            *far_rows,
            grid=(2,),
            in_specs=[tiled(x) for x in near_side[:3]] + [whole(x) for x in near_side[3:]] + [whole(x) for x in far_rows],
            out_specs=[tiled(half_a), whole(half_b)] + [tiled(x) for x in squares] + [whole(x) for x in rows_split],
            flops=6 * n_tall * n_deep * (f_wide + n_wide // 2 * n_high),
        )
        a_kept, b_kept = call(
            functools.partial(kept_kernel, scale_inv, n_high),
            [half_a, half_b],
            table,
            *squared_and_far[:2],
            *near_side[3:],
            *squared_and_far[2:],
            grid=(2,),
            in_specs=[tiled(x) for x in squares] + [whole(x) for x in near_side[3:]] + [whole(x) for x in rows_split],
            out_specs=[tiled(half_a), whole(half_b)],
            flops=6 * n_tall * n_deep * (n_wide // 2 * n_high),
        )

        def over_rows(x, bits):
            for bit in bits:
                half = x.shape[1] // 2
                x = x[:, :half] + swap(x[:, half:], bit)
            return x

        a = over_rows(a_kept + swap(a_sent, high_bits[-1]), high_bits[-2::-1])
        a = a[:tile] + swap_feat(a[tile:], 1)
        b = over_rows(b_kept + swap_feat(b_sent, 1), high_bits[::-1])
        joint = jnp.concatenate([a, b], axis=1)
        step = joint.shape[0] // (n_feat // 2)
        parts = [joint[k * step : (k + 1) * step] for k in range(n_feat // 2)]
        parts = parts[:1] + [swap_feat(part, 2 * k) for k, part in enumerate(parts) if k]
        width = joint.shape[1] // 2
        kept, sent = call(
            functools.partial(divide_kernel, core_at), [f32(step, width)] * 2, table, *parts
        )
        return call(
            functools.partial(assemble_kernel, core_at), [f32(width, 2 * step)], table, kept, swap(sent, 1)
        )[0]

    placed = (P("rows", "feat"), P("feat", "rows"), P("rows", "feat"))
    return jax.shard_map(
        on_device, mesh=mesh, in_specs=placed, out_specs=P("rows", "feat"), check_vma=False
    )
```

```python
import functools

import jax
import jax.numpy as jnp
import numpy as np
from jax import lax
from jax.experimental import pallas as pl
from jax.experimental.pallas import tpu as pltpu
from jax.sharding import PartitionSpec as P

VMEM_BYTES = 40 * 2**20
NEAR_COST, FAR_COST = 40, 0
EARLY, PINS = 2, 2
TIE1, TIE2 = 2, 3
CUTS = 2
ROWS_OVER_ROWS = ((0,), (0,))
LANES_OVER_LANES = ((1,), (1,))


def cycle_of(mesh):
    line = list(mesh.devices[0])
    points = [tuple(d.coords) for d in line]
    moving = [a for a in range(len(points[0])) if len({p[a] for p in points}) > 1]
    if len(moving) != 2:
        return list(range(len(line)))
    inner = min(moving, key=lambda a: len({p[a] for p in points}))
    outer = moving[0] if inner == moving[1] else moving[1]
    at = {(p[outer], p[inner]): i for i, p in enumerate(points)}
    outers, inners = sorted({p[outer] for p in points}), sorted({p[inner] for p in points})
    walk = [at[o, inners[0]] for o in outers]
    for turn, o in enumerate(reversed(outers)):
        walk += [at[o, i] for i in (inners[1:] if turn % 2 == 0 else inners[:0:-1])]
    return walk


def split(a):
    high = a.astype(jnp.bfloat16)
    return high, (a - high.astype(jnp.float32)).astype(jnp.bfloat16)


def dot3(a, b, over=((1,), (0,))):
    def one(x, y):
        return lax.dot_general(x, y, (over, ((), ())), preferred_element_type=jnp.float32)

    return one(a[0], b[0]) + (one(a[0], b[1]) + one(a[1], b[0]))


def call(kernel, out_shape, table, *args, grid=(), in_specs=None, out_specs=None, scratch_shapes=(), flops=0, grant=VMEM_BYTES):
    whole = lambda a: pl.BlockSpec(a.shape, lambda *_: (0,) * len(a.shape))
    outs = list(out_shape)
    return pl.pallas_call(
        kernel,
        out_shape=outs,
        grid_spec=pltpu.PrefetchScalarGridSpec(
            num_scalar_prefetch=1,
            grid=grid or (1,),
            in_specs=in_specs or [whole(a) for a in args],
            out_specs=out_specs or [whole(a) for a in outs],
            scratch_shapes=list(scratch_shapes),
        ),
        compiler_params=pltpu.CompilerParams(vmem_limit_bytes=grant),
        cost_estimate=pl.CostEstimate(flops=flops, bytes_accessed=sum(4 * a.size for a in args), transcendentals=0),
    )(table, *args)


def f32(*shape):
    return jax.ShapeDtypeStruct(shape, jnp.float32)


def bf16(*shape):
    return jax.ShapeDtypeStruct(shape, jnp.bfloat16)


def partial_kernel(core_at, n_tiles, table, *refs):
    tiles, blocks, (out_ref, high_ref, low_ref) = refs[:n_tiles], refs[n_tiles:-3], refs[-3:]
    width = blocks[0].shape[1]
    for core in (0, 1):

        @pl.when((pl.program_id(0) == 0) & (table[core_at] == core))
        def _():
            for k, ref in enumerate(blocks):
                at = (k // 2 * 2 + (k % 2 ^ core)) * width
                high_ref[:, at : at + width], low_ref[:, at : at + width] = split(ref[...])

    rows = jnp.concatenate([ref[...] for ref in tiles], axis=0)
    out_ref[...] = dot3(split(rows), (high_ref[...], low_ref[...]))


def partial_sums(samples, blocks, table, pieces, core_at, cost):
    rows, depth = samples.shape
    width = sum(b.shape[1] for b in blocks)
    height = rows // pieces
    together = max(k for k in (1, 2, 4) if pieces % k == 0 and (k == 1 or height * k <= 384))

    def part(first, steps):
        return call(
            functools.partial(partial_kernel, core_at, together),
            [f32(height * together * steps, width)],
            table,
            *[samples] * together,
            *blocks,
            grid=(steps,),
            in_specs=[
                pl.BlockSpec((height, depth), lambda i, t, k=k: (t[(i + first) * together + k], 0))
                for k in range(together)
            ]
            + [pl.BlockSpec(b.shape, lambda i, t: (0, 0)) for b in blocks],
            out_specs=[pl.BlockSpec((height * together, width), lambda i, t: (i, 0))],
            scratch_shapes=[pltpu.VMEM((depth, width), jnp.bfloat16)] * 2,
            flops=cost * 2 * height * together * steps * depth * width,
        )[0]

    return part(0, 1), part(1, pieces // together - 1)


def near_kernel(order_at, table, *refs):
    *pieces, near_ref, far_ref, projected_ref, high_ref, low_ref, near_high_ref, near_low_ref = refs
    height = pieces[0].shape[0]
    for k, ref in enumerate(pieces):
        rows = slice(k * height, (k + 1) * height)
        near_high_ref[rows, :], near_low_ref[rows, :] = split(ref[...])
    n, height, _ = near_ref.shape
    near, far = [], []
    for half in range(2):
        places = [table[order_at + k] for k in range(half * n // 2, (half + 1) * n // 2)]
        for rows in (slice(0, height // 2), slice(height // 2, height)):
            near += [near_ref[at, rows, :] for at in places]
            far += [far_ref[at, rows, :] for at in places]
    high_ref[...], low_ref[...] = split(jnp.concatenate(far, axis=0))
    near = split(jnp.concatenate(near, axis=0))
    projected_ref[...] = dot3(near, (near_high_ref[...], near_low_ref[...]), LANES_OVER_LANES)


def columns_of(near, far, width, core, highs):
    parts = []
    for h in highs:
        at = core * width if h == 0 else (2 * (h - 1) + core) * width
        parts.append((near if h == 0 else far)[:, at : at + width])
    return parts


def store_moments(ref, squared, scale_inv, columns):
    at = 0
    for high, low in columns:
        width = high.shape[1]
        ref[:, at : at + width] = scale_inv * dot3(squared, (high, low))
        at += width


def sent_kernel(scale_inv, n_high, n_pieces, table, *refs):
    projected_ref, comp_high_ref, comp_low_ref, near_high_ref, near_low_ref, *refs = refs
    pieces, refs = refs[:n_pieces], refs[n_pieces:]
    a0_ref, a1_ref, b0_ref, b1_ref, sq_high_ref, sq_low_ref, far_high_ref, far_low_ref = refs

    @pl.when(pl.program_id(0) == 0)
    def _():
        height = pieces[0].shape[0]
        for k, ref in enumerate(pieces):
            rows = slice(k * height, (k + 1) * height)
            far_high_ref[rows, :], far_low_ref[rows, :] = split(ref[...])

    projected = projected_ref[...] + dot3(
        (comp_high_ref[...], comp_low_ref[...]), (far_high_ref[...], far_low_ref[...]), LANES_OVER_LANES
    )
    squared = split(projected * projected)
    sq_high_ref[...], sq_low_ref[...] = squared
    width, half = near_high_ref.shape[1] // 2, a0_ref.shape[0]

    def columns(core, highs):
        return zip(
            columns_of(near_high_ref, far_high_ref, width, core, highs),
            columns_of(near_low_ref, far_low_ref, width, core, highs),
        )

    for k, ref in enumerate((a0_ref, a1_ref)):
        rows = [x[k * half : (k + 1) * half] for x in squared]
        store_moments(ref, rows, scale_inv, columns(0, range(n_high // 2, n_high)))

    @pl.when(pl.program_id(0) == 1)
    def _():
        for k, ref in enumerate((b0_ref, b1_ref)):
            rows = [x[k * half : (k + 1) * half] for x in squared]
            store_moments(ref, rows, scale_inv, columns(1, range(n_high)))


def kept_kernel(scale_inv, n_high, table, *refs):
    sq_high_ref, sq_low_ref, near_high_ref, near_low_ref, far_high_ref, far_low_ref, *refs = refs
    a0_ref, a1_ref, b0_ref, b1_ref = refs
    width, half = near_high_ref.shape[1] // 2, a0_ref.shape[0]

    def columns(core, highs):
        return zip(
            columns_of(near_high_ref, far_high_ref, width, core, highs),
            columns_of(near_low_ref, far_low_ref, width, core, highs),
        )

    for k, ref in enumerate((a0_ref, a1_ref)):
        rows = [x[k * half : (k + 1) * half, :] for x in (sq_high_ref, sq_low_ref)]
        store_moments(ref, rows, scale_inv, columns(0, range(n_high // 2)))

    @pl.when(pl.program_id(0) == 0)
    def _():
        for k, ref in enumerate((b0_ref, b1_ref)):
            rows = [x[k * half : (k + 1) * half, :] for x in (sq_high_ref, sq_low_ref)]
            store_moments(ref, rows, scale_inv, columns(1, range(n_high)))


def divide_kernel(core_at, table, *refs):
    *parts, kept_ref, sent_ref = refs
    totals = []
    for half in (parts[: len(parts) // 2], parts[len(parts) // 2 :]):
        total = half[0][...]
        for ref in half[1:]:
            total = total + ref[...]
        totals.append(total)
    total = jnp.concatenate(totals, axis=0)
    width = kept_ref.shape[1]
    for core in (0, 1):

        @pl.when(table[core_at] == core)
        def _():
            kept_ref[...] = total[:, core * width : (core + 1) * width]
            sent_ref[...] = total[:, (1 - core) * width : (2 - core) * width]


def assemble_kernel(core_at, table, own_ref, other_ref, out_ref):
    for core in (0, 1):

        @pl.when(table[core_at] == core)
        def _():
            pair = (own_ref[...], other_ref[...])
            out_ref[...] = jnp.concatenate(pair[:: 1 - 2 * core], axis=0).T


def solution(mesh):
    n_rows, n_feat = mesh.shape["rows"], mesh.shape["feat"]
    cycle = cycle_of(mesh)
    place = [cycle.index(i) for i in range(n_feat)]
    n_high = n_rows // 2
    high_bits = [1 << b for b in range(1, n_rows.bit_length() - 1)]
    both = ("rows", "feat")
    streams = [
        [
            (r * n_feat + cycle[i], r * n_feat + cycle[(i + (1 if r % 2 == s else -1)) % n_feat])
            for r in range(n_rows)
            for i in range(n_feat)
        ]
        for s in (0, 1)
    ]
    order = [j for j in range(n_feat) if j % 2 == 0] + [j for j in range(n_feat) if j % 2]
    pieces, reach = n_feat, n_feat // 2
    core_at, order_at = pieces, pieces + 1
    cut = max(1, reach // 2)
    held_order = [0, *range(1, cut + 1), *(n_feat - k for k in range(1, min(cut, reach - 1) + 1))]
    held_order += [*range(cut + 1, reach + 1), *(n_feat - k for k in range(cut + 1, reach))]
    facts = np.zeros((2, n_feat, order_at + n_feat), np.int32)
    for core in (0, 1):
        for f in range(n_feat):
            p, way = place[f], 1 - 2 * core
            for t in range(reach):
                facts[core, f, 2 * t] = (p + way * (reach - t)) % n_feat
                facts[core, f, 2 * t + 1] = (p - way * (reach - 1 - t)) % n_feat
            facts[core, f, core_at] = core
            for k, j in enumerate(order):
                away = way * (p - place[f ^ j]) % n_feat
                facts[core, f, order_at + k] = held_order.index(away)

    def swap(a, bit):
        return lax.ppermute(a, "rows", [(i, i ^ bit) for i in range(n_rows)])

    def swap_feat(a, bit):
        return lax.ppermute(a, "feat", [(i, i ^ bit) for i in range(n_feat)])

    def over_high_bits(own):
        blocks = [own]
        for bit in high_bits:
            blocks += [swap(block, bit) for block in blocks]
        return blocks

    def on_device(samples, whitening, components):
        core = lax.axis_index("rows") % 2
        table = lax.dynamic_slice(
            jnp.asarray(facts), (core, lax.axis_index("feat"), 0), (1, 1, facts.shape[2])
        ).reshape(-1)
        height = samples.shape[0] // pieces

        def rounds(part, first, last, held):
            for t in range(first, last):
                for s in (0, 1):
                    at = 2 * t + s
                    cut_at = part[0].shape[0] // height
                    source, at_row = (part[0], at) if at < cut_at else (part[1], at - cut_at)
                    piece = source[at_row * height : (at_row + 1) * height]
                    if t == 0:
                        held[s] = piece
                    elif at < n_feat:
                        held[s] = lax.ppermute(held[s], both, streams[s]) + piece
            return held

        far = over_high_bits(whitening)[1:]
        near_part = partial_sums(samples, [whitening, swap(whitening, 1)], table, pieces, core_at, NEAR_COST)

        turned = components.T
        turned = turned.reshape(2, turned.shape[0] // 2, -1)
        mine, others = (
            lax.dynamic_index_in_dim(turned, c, keepdims=False) for c in (core, 1 - core)
        )
        others = swap(others, 1)
        first = core == 0
        own = jnp.concatenate([jnp.where(first, mine, others), jnp.where(first, others, mine)], axis=1)
        line, groups = {0: own}, []

        def pass_components(first, last):
            for step in range(first, last):
                line[step] = lax.ppermute(line[step - 1], both, streams[0])
                if step < reach:
                    line[n_feat - step] = lax.ppermute(line[(n_feat - step + 1) % n_feat], both, streams[1])
                if step in (cut, reach):
                    done = sum(g.shape[0] for g in groups)
                    groups.append(jnp.stack([line[away] for away in held_order[done : len(line)]]))

        pass_components(1, 2)
        first_near, line = lax.optimization_barrier((near_part[0], line))
        near_part = (first_near, near_part[1])
        near = rounds(near_part, 0, 1, [None, None])
        for t in range(1, reach):
            if t == EARLY:
                far, near = lax.optimization_barrier((far, near))
                far_blocks = []
                for block in far:
                    far_blocks += [block, swap(block, 1)]
                far_part = partial_sums(samples, far_blocks, table, pieces, core_at, FAR_COST)
            if t < PINS:
                pass_components(t + 1, t + 2)
            near = rounds(near_part, t, t + 1, near)
            if t < PINS:
                near, line = lax.optimization_barrier((near, line))
            if t == EARLY:
                first_far, line = lax.optimization_barrier((far_part[0], line))
                far_part = (first_far, far_part[1])
        near = lax.ppermute(near[0], both, streams[0]) + near[1]
        pass_components(min(PINS + 1, reach + 1), reach + 1)

        held = rounds(far_part, 0, min(TIE1, reach), [None, None])
        over = over_high_bits(groups[0])
        held, over = lax.optimization_barrier((held, over))
        held = rounds(far_part, min(TIE1, reach), min(TIE2, reach), held)
        over = [over] + [over_high_bits(g) for g in groups[1:]]
        held, over = lax.optimization_barrier((held, over))
        near_stack, *far_stacks = [jnp.concatenate(parts) for parts in zip(*over)]
        far_stack = jnp.concatenate(far_stacks, axis=2) if n_high > 2 else far_stacks[0]
        near_rows = [near, swap(near, 1)]
        n_wide, n_tall = near_stack.shape[2], n_feat * near_stack.shape[1]
        f_wide, n_deep = far_stack.shape[2], 2 * height
        near_side = call(
            functools.partial(near_kernel, order_at),
            [f32(n_tall, n_deep), bf16(n_tall, f_wide), bf16(n_tall, f_wide), bf16(n_deep, n_wide), bf16(n_deep, n_wide)],
            table,
            *near_rows,
            near_stack,
            far_stack,
            flops=6 * n_tall * n_deep * n_wide,
        )
        held = rounds(far_part, min(TIE2, reach), reach, held)
        cuts = [slice(k * height // CUTS, (k + 1) * height // CUTS) for k in range(CUTS)]
        arrived = [lax.ppermute(held[0][rows], both, streams[0]) for rows in cuts]
        arrived, near_side = lax.optimization_barrier((arrived, near_side))
        far_rows = [x + held[1][rows] for x, rows in zip(arrived, cuts)]
        far_rows += [swap(x, 1) for x in far_rows]
        scale_inv = float((samples.shape[0] * n_rows) ** -0.5)
        half, wide, n_way = n_tall // 4, n_wide // 2, n_feat // 2
        whole = lambda a: pl.BlockSpec(a.shape, lambda i, t: (0, 0))
        tiled = lambda a: pl.BlockSpec((a.shape[0] // 2, a.shape[1]), lambda i, t: (i, 0))
        half_a, half_b = f32(2 * half, n_high // 2 * wide), f32(half, n_high * wide)
        squares, rows_split = [bf16(n_tall, n_deep)] * 2, [bf16(n_deep, f_wide)] * 2
        *sent, sq_high, sq_low, far_high, far_low = call(
            functools.partial(sent_kernel, scale_inv, n_high, len(far_rows)),
            [half_a] * 2 + [half_b] * 2 + squares + rows_split,
            table,
            *near_side,
            *far_rows,
            grid=(2,),
            in_specs=[tiled(x) for x in near_side[:3]] + [whole(x) for x in near_side[3:]] + [whole(x) for x in far_rows],
            out_specs=[tiled(half_a)] * 2
            + [whole(half_b)] * 2
            + [tiled(x) for x in squares]
            + [whole(x) for x in rows_split],
            flops=6 * n_tall * n_deep * (f_wide + n_wide // 2 * n_high),
        )
        kept = call(
            functools.partial(kept_kernel, scale_inv, n_high),
            [half_a] * 2 + [half_b] * 2,
            table,
            sq_high,
            sq_low,
            *near_side[3:],
            far_high,
            far_low,
            grid=(2,),
            in_specs=[tiled(x) for x in squares] + [whole(x) for x in near_side[3:]] + [whole(x) for x in rows_split],
            out_specs=[tiled(half_a)] * 2 + [whole(half_b)] * 2,
            flops=6 * n_tall * n_deep * (n_wide // 2 * n_high),
        )

        def over_rows(x, bits):
            for bit in bits:
                cols = x.shape[1] // 2
                x = x[:, :cols] + swap(x[:, cols:], bit)
            return x

        def over_chips(a_sent, b_sent, a_kept, b_kept):
            a = over_rows(a_kept + swap(a_sent, high_bits[-1]), high_bits[-2::-1])
            a = a[:half] + swap_feat(a[half:], 1)
            b = over_rows(b_kept + swap_feat(b_sent, 1), high_bits[::-1])
            joint = jnp.concatenate([a, b], axis=1)
            step = half // n_way
            parts = [joint[k * step : (k + 1) * step] for k in range(n_way)]
            return parts[:1] + [swap_feat(part, 2 * k) for k, part in enumerate(parts) if k]

        parts = over_chips(*sent[::2], *kept[::2]) + over_chips(*sent[1::2], *kept[1::2])
        height = 2 * half // n_way
        kept, sent = call(functools.partial(divide_kernel, core_at), [f32(height, wide)] * 2, table, *parts)
        return call(
            functools.partial(assemble_kernel, core_at), [f32(wide, 2 * height)], table, kept, swap(sent, 1)
        )[0]

    placed = (P("rows", "feat"), P("feat", "rows"), P("rows", "feat"))
    return jax.shard_map(
        on_device, mesh=mesh, in_specs=placed, out_specs=P("rows", "feat"), check_vma=False
    )
```

```python
import functools

import jax
import jax.numpy as jnp
import numpy as np
from jax import lax
from jax.experimental import pallas as pl
from jax.experimental.pallas import tpu as pltpu
from jax.sharding import PartitionSpec as P

VMEM_BYTES = 40 * 2**20
NEAR_COST, FAR_COST = 40, 0
EARLY, PINS = 2, 2
TIE1, TIE2 = 2, 3
ROWS_OVER_ROWS = ((0,), (0,))
LANES_OVER_LANES = ((1,), (1,))


def cycle_of(mesh):
    line = list(mesh.devices[0])
    points = [tuple(d.coords) for d in line]
    moving = [a for a in range(len(points[0])) if len({p[a] for p in points}) > 1]
    if len(moving) != 2:
        return list(range(len(line)))
    inner = min(moving, key=lambda a: len({p[a] for p in points}))
    outer = moving[0] if inner == moving[1] else moving[1]
    at = {(p[outer], p[inner]): i for i, p in enumerate(points)}
    outers, inners = sorted({p[outer] for p in points}), sorted({p[inner] for p in points})
    walk = [at[o, inners[0]] for o in outers]
    for turn, o in enumerate(reversed(outers)):
        walk += [at[o, i] for i in (inners[1:] if turn % 2 == 0 else inners[:0:-1])]
    return walk


def split(a):
    high = a.astype(jnp.bfloat16)
    return high, (a - high.astype(jnp.float32)).astype(jnp.bfloat16)


def dot3(a, b, over=((1,), (0,))):
    def one(x, y):
        return lax.dot_general(x, y, (over, ((), ())), preferred_element_type=jnp.float32)

    return one(a[0], b[0]) + (one(a[0], b[1]) + one(a[1], b[0]))


def call(kernel, out_shape, table, *args, grid=(), in_specs=None, out_specs=None, scratch_shapes=(), flops=0, grant=VMEM_BYTES):
    whole = lambda a: pl.BlockSpec(a.shape, lambda *_: (0,) * len(a.shape))
    outs = list(out_shape)
    return pl.pallas_call(
        kernel,
        out_shape=outs,
        grid_spec=pltpu.PrefetchScalarGridSpec(
            num_scalar_prefetch=1,
            grid=grid or (1,),
            in_specs=in_specs or [whole(a) for a in args],
            out_specs=out_specs or [whole(a) for a in outs],
            scratch_shapes=list(scratch_shapes),
        ),
        compiler_params=pltpu.CompilerParams(vmem_limit_bytes=grant),
        cost_estimate=pl.CostEstimate(flops=flops, bytes_accessed=sum(4 * a.size for a in args), transcendentals=0),
    )(table, *args)


def f32(*shape):
    return jax.ShapeDtypeStruct(shape, jnp.float32)


def bf16(*shape):
    return jax.ShapeDtypeStruct(shape, jnp.bfloat16)


def partial_kernel(core_at, n_tiles, table, *refs):
    tiles, blocks, (out_ref, high_ref, low_ref) = refs[:n_tiles], refs[n_tiles:-3], refs[-3:]
    width = blocks[0].shape[1]
    for core in (0, 1):

        @pl.when((pl.program_id(0) == 0) & (table[core_at] == core))
        def _():
            for k, ref in enumerate(blocks):
                at = (k // 2 * 2 + (k % 2 ^ core)) * width
                high_ref[:, at : at + width], low_ref[:, at : at + width] = split(ref[...])

    rows = jnp.concatenate([ref[...] for ref in tiles], axis=0)
    out_ref[...] = dot3(split(rows), (high_ref[...], low_ref[...]))


def partial_sums(samples, blocks, table, pieces, core_at, cost):
    rows, depth = samples.shape
    width = sum(b.shape[1] for b in blocks)
    height = rows // pieces
    together = max(k for k in (1, 2, 4) if pieces % k == 0 and (k == 1 or height * k <= 384))

    def part(first, steps):
        return call(
            functools.partial(partial_kernel, core_at, together),
            [f32(height * together * steps, width)],
            table,
            *[samples] * together,
            *blocks,
            grid=(steps,),
            in_specs=[
                pl.BlockSpec((height, depth), lambda i, t, k=k: (t[(i + first) * together + k], 0))
                for k in range(together)
            ]
            + [pl.BlockSpec(b.shape, lambda i, t: (0, 0)) for b in blocks],
            out_specs=[pl.BlockSpec((height * together, width), lambda i, t: (i, 0))],
            scratch_shapes=[pltpu.VMEM((depth, width), jnp.bfloat16)] * 2,
            flops=cost * 2 * height * together * steps * depth * width,
        )[0]

    return part(0, 1), part(1, pieces // together - 1)


def near_kernel(order_at, table, *refs):
    *pieces, near_ref, far_ref, projected_ref, high_ref, low_ref, near_high_ref, near_low_ref = refs
    height = pieces[0].shape[0]
    for k, ref in enumerate(pieces):
        rows = slice(k * height, (k + 1) * height)
        near_high_ref[rows, :], near_low_ref[rows, :] = split(ref[...])
    n, height, _ = near_ref.shape
    near, far = [], []
    for half in range(2):
        places = [table[order_at + k] for k in range(half * n // 2, (half + 1) * n // 2)]
        for rows in (slice(0, height // 2), slice(height // 2, height)):
            near += [near_ref[at, rows, :] for at in places]
            far += [far_ref[at, rows, :] for at in places]
    high_ref[...], low_ref[...] = split(jnp.concatenate(far, axis=0))
    near = split(jnp.concatenate(near, axis=0))
    projected_ref[...] = dot3(near, (near_high_ref[...], near_low_ref[...]), LANES_OVER_LANES)


def columns_of(near, far, width, core, highs):
    parts = []
    for h in highs:
        at = core * width if h == 0 else (2 * (h - 1) + core) * width
        parts.append((near if h == 0 else far)[:, at : at + width])
    return parts


def store_moments(ref, squared, scale_inv, columns):
    at = 0
    for high, low in columns:
        width = high.shape[1]
        ref[:, at : at + width] = scale_inv * dot3(squared, (high, low))
        at += width


def sent_kernel(scale_inv, n_high, n_pieces, table, *refs):
    projected_ref, comp_high_ref, comp_low_ref, near_high_ref, near_low_ref, *refs = refs
    pieces, refs = refs[:n_pieces], refs[n_pieces:]
    a0_ref, a1_ref, b0_ref, b1_ref, sq_high_ref, sq_low_ref, far_high_ref, far_low_ref = refs

    @pl.when(pl.program_id(0) == 0)
    def _():
        height = pieces[0].shape[0]
        for k, ref in enumerate(pieces):
            rows = slice(k * height, (k + 1) * height)
            far_high_ref[rows, :], far_low_ref[rows, :] = split(ref[...])

    projected = projected_ref[...] + dot3(
        (comp_high_ref[...], comp_low_ref[...]), (far_high_ref[...], far_low_ref[...]), LANES_OVER_LANES
    )
    squared = split(projected * projected)
    sq_high_ref[...], sq_low_ref[...] = squared
    width, half = near_high_ref.shape[1] // 2, a0_ref.shape[0]

    def columns(core, highs):
        return zip(
            columns_of(near_high_ref, far_high_ref, width, core, highs),
            columns_of(near_low_ref, far_low_ref, width, core, highs),
        )

    for k, ref in enumerate((a0_ref, a1_ref)):
        rows = [x[k * half : (k + 1) * half] for x in squared]
        store_moments(ref, rows, scale_inv, columns(0, range(n_high // 2, n_high)))

    @pl.when(pl.program_id(0) == 1)
    def _():
        for k, ref in enumerate((b0_ref, b1_ref)):
            rows = [x[k * half : (k + 1) * half] for x in squared]
            store_moments(ref, rows, scale_inv, columns(1, range(n_high)))


def kept_kernel(scale_inv, n_high, table, *refs):
    sq_high_ref, sq_low_ref, near_high_ref, near_low_ref, far_high_ref, far_low_ref, *refs = refs
    a0_ref, a1_ref, b0_ref, b1_ref = refs
    width, half = near_high_ref.shape[1] // 2, a0_ref.shape[0]

    def columns(core, highs):
        return zip(
            columns_of(near_high_ref, far_high_ref, width, core, highs),
            columns_of(near_low_ref, far_low_ref, width, core, highs),
        )

    for k, ref in enumerate((a0_ref, a1_ref)):
        rows = [x[k * half : (k + 1) * half, :] for x in (sq_high_ref, sq_low_ref)]
        store_moments(ref, rows, scale_inv, columns(0, range(n_high // 2)))

    @pl.when(pl.program_id(0) == 0)
    def _():
        for k, ref in enumerate((b0_ref, b1_ref)):
            rows = [x[k * half : (k + 1) * half, :] for x in (sq_high_ref, sq_low_ref)]
            store_moments(ref, rows, scale_inv, columns(1, range(n_high)))


def divide_kernel(core_at, table, *refs):
    *parts, kept_ref, sent_ref = refs
    totals = []
    for half in (parts[: len(parts) // 2], parts[len(parts) // 2 :]):
        total = half[0][...]
        for ref in half[1:]:
            total = total + ref[...]
        totals.append(total)
    total = jnp.concatenate(totals, axis=0)
    width = kept_ref.shape[1]
    for core in (0, 1):

        @pl.when(table[core_at] == core)
        def _():
            kept_ref[...] = total[:, core * width : (core + 1) * width]
            sent_ref[...] = total[:, (1 - core) * width : (2 - core) * width]


def assemble_kernel(core_at, table, own_ref, other_ref, out_ref):
    for core in (0, 1):

        @pl.when(table[core_at] == core)
        def _():
            pair = (own_ref[...], other_ref[...])
            out_ref[...] = jnp.concatenate(pair[:: 1 - 2 * core], axis=0).T


def solution(mesh):
    n_rows, n_feat = mesh.shape["rows"], mesh.shape["feat"]
    cycle = cycle_of(mesh)
    place = [cycle.index(i) for i in range(n_feat)]
    n_high = n_rows // 2
    high_bits = [1 << b for b in range(1, n_rows.bit_length() - 1)]
    both = ("rows", "feat")
    streams = [
        [
            (r * n_feat + cycle[i], r * n_feat + cycle[(i + (1 if r % 2 == s else -1)) % n_feat])
            for r in range(n_rows)
            for i in range(n_feat)
        ]
        for s in (0, 1)
    ]
    order = [j for j in range(n_feat) if j % 2 == 0] + [j for j in range(n_feat) if j % 2]
    pieces, reach = n_feat, n_feat // 2
    core_at, order_at = pieces, pieces + 1
    cut = max(1, reach // 2)
    held_order = [0, *range(1, cut + 1), *(n_feat - k for k in range(1, min(cut, reach - 1) + 1))]
    held_order += [*range(cut + 1, reach + 1), *(n_feat - k for k in range(cut + 1, reach))]
    facts = np.zeros((2, n_feat, order_at + n_feat), np.int32)
    for core in (0, 1):
        for f in range(n_feat):
            p, way = place[f], 1 - 2 * core
            for t in range(reach):
                facts[core, f, 2 * t] = (p + way * (reach - t)) % n_feat
                facts[core, f, 2 * t + 1] = (p - way * (reach - 1 - t)) % n_feat
            facts[core, f, core_at] = core
            for k, j in enumerate(order):
                away = way * (p - place[f ^ j]) % n_feat
                facts[core, f, order_at + k] = held_order.index(away)

    def swap(a, bit):
        return lax.ppermute(a, "rows", [(i, i ^ bit) for i in range(n_rows)])

    def swap_feat(a, bit):
        return lax.ppermute(a, "feat", [(i, i ^ bit) for i in range(n_feat)])

    def over_high_bits(own):
        blocks = [own]
        for bit in high_bits:
            blocks += [swap(block, bit) for block in blocks]
        return blocks

    def on_device(samples, whitening, components):
        core = lax.axis_index("rows") % 2
        table = lax.dynamic_slice(
            jnp.asarray(facts), (core, lax.axis_index("feat"), 0), (1, 1, facts.shape[2])
        ).reshape(-1)
        height = samples.shape[0] // pieces

        def rounds(part, first, last, held):
            for t in range(first, last):
                for s in (0, 1):
                    at = 2 * t + s
                    cut_at = part[0].shape[0] // height
                    source, at_row = (part[0], at) if at < cut_at else (part[1], at - cut_at)
                    piece = source[at_row * height : (at_row + 1) * height]
                    if t == 0:
                        held[s] = piece
                    elif at < n_feat:
                        held[s] = lax.ppermute(held[s], both, streams[s]) + piece
            return held

        far = over_high_bits(whitening)[1:]
        near_part = partial_sums(samples, [whitening, swap(whitening, 1)], table, pieces, core_at, NEAR_COST)

        turned = components.T
        turned = turned.reshape(2, turned.shape[0] // 2, -1)
        mine, others = (
            lax.dynamic_index_in_dim(turned, c, keepdims=False) for c in (core, 1 - core)
        )
        others = swap(others, 1)
        first = core == 0
        own = jnp.concatenate([jnp.where(first, mine, others), jnp.where(first, others, mine)], axis=1)
        line, groups = {0: own}, []

        def pass_components(first, last):
            for step in range(first, last):
                line[step] = lax.ppermute(line[step - 1], both, streams[0])
                if step < reach:
                    line[n_feat - step] = lax.ppermute(line[(n_feat - step + 1) % n_feat], both, streams[1])
                if step in (cut, reach):
                    done = sum(g.shape[0] for g in groups)
                    groups.append(jnp.stack([line[away] for away in held_order[done : len(line)]]))

        pass_components(1, 2)
        first_near, line = lax.optimization_barrier((near_part[0], line))
        near_part = (first_near, near_part[1])
        near = rounds(near_part, 0, 1, [None, None])
        later_near, line = lax.optimization_barrier((near_part[1], line))
        near_part = (near_part[0], later_near)
        for t in range(1, reach):
            if t == EARLY:
                far, near = lax.optimization_barrier((far, near))
                far_blocks = []
                for block in far:
                    far_blocks += [block, swap(block, 1)]
                far_part = partial_sums(samples, far_blocks, table, pieces, core_at, FAR_COST)
            if t < PINS:
                pass_components(t + 1, t + 2)
            near = rounds(near_part, t, t + 1, near)
            if t < PINS:
                near, line = lax.optimization_barrier((near, line))
            if t == EARLY:
                first_far, line = lax.optimization_barrier((far_part[0], line))
                far_part = (first_far, far_part[1])
        near = lax.ppermute(near[0], both, streams[0]) + near[1]
        pass_components(min(PINS + 1, reach + 1), reach + 1)

        held = rounds(far_part, 0, min(TIE1, reach), [None, None])
        over = over_high_bits(groups[0])
        held, over = lax.optimization_barrier((held, over))
        held = rounds(far_part, min(TIE1, reach), min(TIE2, reach), held)
        over = [over] + [over_high_bits(g) for g in groups[1:]]
        held, over = lax.optimization_barrier((held, over))
        near_stack, *far_stacks = [jnp.concatenate(parts) for parts in zip(*over)]
        far_stack = jnp.concatenate(far_stacks, axis=2) if n_high > 2 else far_stacks[0]
        near_rows = [near, swap(near, 1)]
        n_wide, n_tall = near_stack.shape[2], n_feat * near_stack.shape[1]
        f_wide, n_deep = far_stack.shape[2], 2 * height
        near_side = call(
            functools.partial(near_kernel, order_at),
            [f32(n_tall, n_deep), bf16(n_tall, f_wide), bf16(n_tall, f_wide), bf16(n_deep, n_wide), bf16(n_deep, n_wide)],
            table,
            *near_rows,
            near_stack,
            far_stack,
            flops=6 * n_tall * n_deep * n_wide,
        )
        held = rounds(far_part, min(TIE2, reach), reach, held)
        arrived = lax.ppermute(held[0], both, streams[0])
        arrived, near_side = lax.optimization_barrier((arrived, near_side))
        far_rows = [arrived + held[1]]
        far_rows += [swap(x, 1) for x in far_rows]
        scale_inv = float((samples.shape[0] * n_rows) ** -0.5)
        half, wide, n_way = n_tall // 4, n_wide // 2, n_feat // 2
        whole = lambda a: pl.BlockSpec(a.shape, lambda i, t: (0, 0))
        tiled = lambda a: pl.BlockSpec((a.shape[0] // 2, a.shape[1]), lambda i, t: (i, 0))
        half_a, half_b = f32(2 * half, n_high // 2 * wide), f32(half, n_high * wide)
        squares, rows_split = [bf16(n_tall, n_deep)] * 2, [bf16(n_deep, f_wide)] * 2
        *sent, sq_high, sq_low, far_high, far_low = call(
            functools.partial(sent_kernel, scale_inv, n_high, len(far_rows)),
            [half_a] * 2 + [half_b] * 2 + squares + rows_split,
            table,
            *near_side,
            *far_rows,
            grid=(2,),
            in_specs=[tiled(x) for x in near_side[:3]] + [whole(x) for x in near_side[3:]] + [whole(x) for x in far_rows],
            out_specs=[tiled(half_a)] * 2
            + [whole(half_b)] * 2
            + [tiled(x) for x in squares]
            + [whole(x) for x in rows_split],
            flops=6 * n_tall * n_deep * (f_wide + n_wide // 2 * n_high),
        )
        kept = call(
            functools.partial(kept_kernel, scale_inv, n_high),
            [half_a] * 2 + [half_b] * 2,
            table,
            sq_high,
            sq_low,
            *near_side[3:],
            far_high,
            far_low,
            grid=(2,),
            in_specs=[tiled(x) for x in squares] + [whole(x) for x in near_side[3:]] + [whole(x) for x in rows_split],
            out_specs=[tiled(half_a)] * 2 + [whole(half_b)] * 2,
            flops=6 * n_tall * n_deep * (n_wide // 2 * n_high),
        )

        def over_rows(x, bits):
            for bit in bits:
                cols = x.shape[1] // 2
                x = x[:, :cols] + swap(x[:, cols:], bit)
            return x

        def over_chips(a_sent, b_sent, a_kept, b_kept):
            a = over_rows(a_kept + swap(a_sent, high_bits[-1]), high_bits[-2::-1])
            a = a[:half] + swap_feat(a[half:], 1)
            b = over_rows(b_kept + swap_feat(b_sent, 1), high_bits[::-1])
            joint = jnp.concatenate([a, b], axis=1)
            step = half // n_way
            parts = [joint[k * step : (k + 1) * step] for k in range(n_way)]
            return parts[:1] + [swap_feat(part, 2 * k) for k, part in enumerate(parts) if k]

        parts = over_chips(*sent[::2], *kept[::2]) + over_chips(*sent[1::2], *kept[1::2])
        height = 2 * half // n_way
        kept, sent = call(functools.partial(divide_kernel, core_at), [f32(height, wide)] * 2, table, *parts)
        return call(
            functools.partial(assemble_kernel, core_at), [f32(wide, 2 * height)], table, kept, swap(sent, 1)
        )[0]

    placed = (P("rows", "feat"), P("feat", "rows"), P("rows", "feat"))
    return jax.shard_map(
        on_device, mesh=mesh, in_specs=placed, out_specs=P("rows", "feat"), check_vma=False
    )
```

```python
import functools

import jax
import jax.numpy as jnp
import numpy as np
from jax import lax
from jax.experimental import pallas as pl
from jax.experimental.pallas import tpu as pltpu
from jax.sharding import PartitionSpec as P

VMEM_BYTES = 40 * 2**20
NEAR_COST, FAR_COST = 40, 0
EARLY, PINS = 2, 2
TIE1, TIE2 = 2, 3
ROWS_OVER_ROWS = ((0,), (0,))
LANES_OVER_LANES = ((1,), (1,))


def cycle_of(mesh):
    line = list(mesh.devices[0])
    points = [tuple(d.coords) for d in line]
    moving = [a for a in range(len(points[0])) if len({p[a] for p in points}) > 1]
    if len(moving) != 2:
        return list(range(len(line)))
    inner = min(moving, key=lambda a: len({p[a] for p in points}))
    outer = moving[0] if inner == moving[1] else moving[1]
    at = {(p[outer], p[inner]): i for i, p in enumerate(points)}
    outers, inners = sorted({p[outer] for p in points}), sorted({p[inner] for p in points})
    walk = [at[o, inners[0]] for o in outers]
    for turn, o in enumerate(reversed(outers)):
        walk += [at[o, i] for i in (inners[1:] if turn % 2 == 0 else inners[:0:-1])]
    return walk


def split(a):
    high = a.astype(jnp.bfloat16)
    return high, (a - high.astype(jnp.float32)).astype(jnp.bfloat16)


def dot3(a, b, over=((1,), (0,))):
    def one(x, y):
        return lax.dot_general(x, y, (over, ((), ())), preferred_element_type=jnp.float32)

    return one(a[0], b[0]) + (one(a[0], b[1]) + one(a[1], b[0]))


def call(kernel, out_shape, table, *args, grid=(), in_specs=None, out_specs=None, scratch_shapes=(), flops=0, grant=VMEM_BYTES):
    whole = lambda a: pl.BlockSpec(a.shape, lambda *_: (0,) * len(a.shape))
    outs = list(out_shape)
    return pl.pallas_call(
        kernel,
        out_shape=outs,
        grid_spec=pltpu.PrefetchScalarGridSpec(
            num_scalar_prefetch=1,
            grid=grid or (1,),
            in_specs=in_specs or [whole(a) for a in args],
            out_specs=out_specs or [whole(a) for a in outs],
            scratch_shapes=list(scratch_shapes),
        ),
        compiler_params=pltpu.CompilerParams(vmem_limit_bytes=grant),
        cost_estimate=pl.CostEstimate(flops=flops, bytes_accessed=sum(4 * a.size for a in args), transcendentals=0),
    )(table, *args)


def f32(*shape):
    return jax.ShapeDtypeStruct(shape, jnp.float32)


def bf16(*shape):
    return jax.ShapeDtypeStruct(shape, jnp.bfloat16)


def partial_kernel(core_at, n_tiles, table, *refs):
    tiles, blocks, (out_ref, high_ref, low_ref) = refs[:n_tiles], refs[n_tiles:-3], refs[-3:]
    width = blocks[0].shape[1]
    for core in (0, 1):

        @pl.when((pl.program_id(0) == 0) & (table[core_at] == core))
        def _():
            for k, ref in enumerate(blocks):
                at = (k // 2 * 2 + (k % 2 ^ core)) * width
                high_ref[:, at : at + width], low_ref[:, at : at + width] = split(ref[...])

    rows = jnp.concatenate([ref[...] for ref in tiles], axis=0)
    out_ref[...] = dot3(split(rows), (high_ref[...], low_ref[...]))


def partial_sums(samples, blocks, table, pieces, core_at, cost):
    rows, depth = samples.shape
    width = sum(b.shape[1] for b in blocks)
    height = rows // pieces
    together = max(k for k in (1, 2, 4) if pieces % k == 0 and (k == 1 or height * k <= 384))

    def part(first, steps):
        return call(
            functools.partial(partial_kernel, core_at, together),
            [f32(height * together * steps, width)],
            table,
            *[samples] * together,
            *blocks,
            grid=(steps,),
            in_specs=[
                pl.BlockSpec((height, depth), lambda i, t, k=k: (t[(i + first) * together + k], 0))
                for k in range(together)
            ]
            + [pl.BlockSpec(b.shape, lambda i, t: (0, 0)) for b in blocks],
            out_specs=[pl.BlockSpec((height * together, width), lambda i, t: (i, 0))],
            scratch_shapes=[pltpu.VMEM((depth, width), jnp.bfloat16)] * 2,
            flops=cost * 2 * height * together * steps * depth * width,
        )[0]

    if cost:
        rows_of = [lax.dynamic_slice_in_dim(samples, table[k] * height, height, 0) for k in range(together)]
        first = call(
            functools.partial(partial_kernel, core_at, together),
            [f32(height * together, width)],
            table,
            *rows_of,
            *blocks,
            scratch_shapes=[pltpu.VMEM((depth, width), jnp.bfloat16)] * 2,
            flops=cost * 2 * height * together * depth * width,
        )[0]
    else:
        first = part(0, 1)
    return first, part(1, pieces // together - 1)


def near_kernel(order_at, table, *refs):
    *pieces, near_ref, far_ref, projected_ref, high_ref, low_ref, near_high_ref, near_low_ref = refs
    height = pieces[0].shape[0]
    for k, ref in enumerate(pieces):
        rows = slice(k * height, (k + 1) * height)
        near_high_ref[rows, :], near_low_ref[rows, :] = split(ref[...])
    n, height, _ = near_ref.shape
    near, far = [], []
    for half in range(2):
        places = [table[order_at + k] for k in range(half * n // 2, (half + 1) * n // 2)]
        for rows in (slice(0, height // 2), slice(height // 2, height)):
            near += [near_ref[at, rows, :] for at in places]
            far += [far_ref[at, rows, :] for at in places]
    high_ref[...], low_ref[...] = split(jnp.concatenate(far, axis=0))
    near = split(jnp.concatenate(near, axis=0))
    projected_ref[...] = dot3(near, (near_high_ref[...], near_low_ref[...]), LANES_OVER_LANES)


def columns_of(near, far, width, core, highs):
    parts = []
    for h in highs:
        at = core * width if h == 0 else (2 * (h - 1) + core) * width
        parts.append((near if h == 0 else far)[:, at : at + width])
    return parts


def store_moments(ref, squared, scale_inv, columns):
    at = 0
    for high, low in columns:
        width = high.shape[1]
        ref[:, at : at + width] = scale_inv * dot3(squared, (high, low))
        at += width


def sent_kernel(scale_inv, n_high, n_pieces, table, *refs):
    projected_ref, comp_high_ref, comp_low_ref, near_high_ref, near_low_ref, *refs = refs
    pieces, refs = refs[:n_pieces], refs[n_pieces:]
    a0_ref, a1_ref, b0_ref, b1_ref, sq_high_ref, sq_low_ref, far_high_ref, far_low_ref = refs

    @pl.when(pl.program_id(0) == 0)
    def _():
        height = pieces[0].shape[0]
        for k, ref in enumerate(pieces):
            rows = slice(k * height, (k + 1) * height)
            far_high_ref[rows, :], far_low_ref[rows, :] = split(ref[...])

    projected = projected_ref[...] + dot3(
        (comp_high_ref[...], comp_low_ref[...]), (far_high_ref[...], far_low_ref[...]), LANES_OVER_LANES
    )
    squared = split(projected * projected)
    sq_high_ref[...], sq_low_ref[...] = squared
    width, half = near_high_ref.shape[1] // 2, a0_ref.shape[0]

    def columns(core, highs):
        return zip(
            columns_of(near_high_ref, far_high_ref, width, core, highs),
            columns_of(near_low_ref, far_low_ref, width, core, highs),
        )

    for k, ref in enumerate((a0_ref, a1_ref)):
        rows = [x[k * half : (k + 1) * half] for x in squared]
        store_moments(ref, rows, scale_inv, columns(0, range(n_high // 2, n_high)))

    @pl.when(pl.program_id(0) == 1)
    def _():
        for k, ref in enumerate((b0_ref, b1_ref)):
            rows = [x[k * half : (k + 1) * half] for x in squared]
            store_moments(ref, rows, scale_inv, columns(1, range(n_high)))


def kept_kernel(scale_inv, n_high, table, *refs):
    sq_high_ref, sq_low_ref, near_high_ref, near_low_ref, far_high_ref, far_low_ref, *refs = refs
    a0_ref, a1_ref, b0_ref, b1_ref = refs
    width, half = near_high_ref.shape[1] // 2, a0_ref.shape[0]

    def columns(core, highs):
        return zip(
            columns_of(near_high_ref, far_high_ref, width, core, highs),
            columns_of(near_low_ref, far_low_ref, width, core, highs),
        )

    for k, ref in enumerate((a0_ref, a1_ref)):
        rows = [x[k * half : (k + 1) * half, :] for x in (sq_high_ref, sq_low_ref)]
        store_moments(ref, rows, scale_inv, columns(0, range(n_high // 2)))

    @pl.when(pl.program_id(0) == 0)
    def _():
        for k, ref in enumerate((b0_ref, b1_ref)):
            rows = [x[k * half : (k + 1) * half, :] for x in (sq_high_ref, sq_low_ref)]
            store_moments(ref, rows, scale_inv, columns(1, range(n_high)))


def divide_kernel(core_at, table, *refs):
    *parts, kept_ref, sent_ref = refs
    totals = []
    for half in (parts[: len(parts) // 2], parts[len(parts) // 2 :]):
        total = half[0][...]
        for ref in half[1:]:
            total = total + ref[...]
        totals.append(total)
    total = jnp.concatenate(totals, axis=0)
    width = kept_ref.shape[1]
    for core in (0, 1):

        @pl.when(table[core_at] == core)
        def _():
            kept_ref[...] = total[:, core * width : (core + 1) * width]
            sent_ref[...] = total[:, (1 - core) * width : (2 - core) * width]


def assemble_kernel(core_at, table, own_ref, other_ref, out_ref):
    for core in (0, 1):

        @pl.when(table[core_at] == core)
        def _():
            pair = (own_ref[...], other_ref[...])
            out_ref[...] = jnp.concatenate(pair[:: 1 - 2 * core], axis=0).T


def solution(mesh):
    n_rows, n_feat = mesh.shape["rows"], mesh.shape["feat"]
    cycle = cycle_of(mesh)
    place = [cycle.index(i) for i in range(n_feat)]
    n_high = n_rows // 2
    high_bits = [1 << b for b in range(1, n_rows.bit_length() - 1)]
    both = ("rows", "feat")
    streams = [
        [
            (r * n_feat + cycle[i], r * n_feat + cycle[(i + (1 if r % 2 == s else -1)) % n_feat])
            for r in range(n_rows)
            for i in range(n_feat)
        ]
        for s in (0, 1)
    ]
    order = [j for j in range(n_feat) if j % 2 == 0] + [j for j in range(n_feat) if j % 2]
    pieces, reach = n_feat, n_feat // 2
    core_at, order_at = pieces, pieces + 1
    cut = max(1, reach // 2)
    held_order = [0, *range(1, cut + 1), *(n_feat - k for k in range(1, min(cut, reach - 1) + 1))]
    held_order += [*range(cut + 1, reach + 1), *(n_feat - k for k in range(cut + 1, reach))]
    facts = np.zeros((2, n_feat, order_at + n_feat), np.int32)
    for core in (0, 1):
        for f in range(n_feat):
            p, way = place[f], 1 - 2 * core
            for t in range(reach):
                facts[core, f, 2 * t] = (p + way * (reach - t)) % n_feat
                facts[core, f, 2 * t + 1] = (p - way * (reach - 1 - t)) % n_feat
            facts[core, f, core_at] = core
            for k, j in enumerate(order):
                away = way * (p - place[f ^ j]) % n_feat
                facts[core, f, order_at + k] = held_order.index(away)

    def swap(a, bit):
        return lax.ppermute(a, "rows", [(i, i ^ bit) for i in range(n_rows)])

    def swap_feat(a, bit):
        return lax.ppermute(a, "feat", [(i, i ^ bit) for i in range(n_feat)])

    def over_high_bits(own):
        blocks = [own]
        for bit in high_bits:
            blocks += [swap(block, bit) for block in blocks]
        return blocks

    def on_device(samples, whitening, components):
        core = lax.axis_index("rows") % 2
        table = lax.dynamic_slice(
            jnp.asarray(facts), (core, lax.axis_index("feat"), 0), (1, 1, facts.shape[2])
        ).reshape(-1)
        height = samples.shape[0] // pieces

        def rounds(part, first, last, held):
            for t in range(first, last):
                for s in (0, 1):
                    at = 2 * t + s
                    cut_at = part[0].shape[0] // height
                    source, at_row = (part[0], at) if at < cut_at else (part[1], at - cut_at)
                    piece = source[at_row * height : (at_row + 1) * height]
                    if t == 0:
                        held[s] = piece
                    elif at < n_feat:
                        held[s] = lax.ppermute(held[s], both, streams[s]) + piece
            return held

        far = over_high_bits(whitening)[1:]
        near_part = partial_sums(samples, [whitening, swap(whitening, 1)], table, pieces, core_at, NEAR_COST)

        turned = components.T
        turned = turned.reshape(2, turned.shape[0] // 2, -1)
        mine, others = (
            lax.dynamic_index_in_dim(turned, c, keepdims=False) for c in (core, 1 - core)
        )
        others = swap(others, 1)
        first = core == 0
        own = jnp.concatenate([jnp.where(first, mine, others), jnp.where(first, others, mine)], axis=1)
        line, groups = {0: own}, []

        def pass_components(first, last):
            for step in range(first, last):
                line[step] = lax.ppermute(line[step - 1], both, streams[0])
                if step < reach:
                    line[n_feat - step] = lax.ppermute(line[(n_feat - step + 1) % n_feat], both, streams[1])
                if step in (cut, reach):
                    done = sum(g.shape[0] for g in groups)
                    groups.append(jnp.stack([line[away] for away in held_order[done : len(line)]]))

        pass_components(1, 2)
        near = rounds(near_part, 0, 1, [None, None])
        later_near, line = lax.optimization_barrier((near_part[1], line))
        near_part = (near_part[0], later_near)
        for t in range(1, reach):
            if t == EARLY:
                far, near = lax.optimization_barrier((far, near))
                far_blocks = []
                for block in far:
                    far_blocks += [block, swap(block, 1)]
                far_part = partial_sums(samples, far_blocks, table, pieces, core_at, FAR_COST)
            if t < PINS:
                pass_components(t + 1, t + 2)
            near = rounds(near_part, t, t + 1, near)
            if t < PINS:
                near, line = lax.optimization_barrier((near, line))
            if t == EARLY:
                first_far, line = lax.optimization_barrier((far_part[0], line))
                far_part = (first_far, far_part[1])
        near = lax.ppermute(near[0], both, streams[0]) + near[1]
        pass_components(min(PINS + 1, reach + 1), reach + 1)

        held = rounds(far_part, 0, min(TIE1, reach), [None, None])
        over = over_high_bits(groups[0])
        held, over = lax.optimization_barrier((held, over))
        held = rounds(far_part, min(TIE1, reach), min(TIE2, reach), held)
        over = [over] + [over_high_bits(g) for g in groups[1:]]
        held, over = lax.optimization_barrier((held, over))
        near_stack, *far_stacks = [jnp.concatenate(parts) for parts in zip(*over)]
        far_stack = jnp.concatenate(far_stacks, axis=2) if n_high > 2 else far_stacks[0]
        near_rows = [near, swap(near, 1)]
        n_wide, n_tall = near_stack.shape[2], n_feat * near_stack.shape[1]
        f_wide, n_deep = far_stack.shape[2], 2 * height
        near_side = call(
            functools.partial(near_kernel, order_at),
            [f32(n_tall, n_deep), bf16(n_tall, f_wide), bf16(n_tall, f_wide), bf16(n_deep, n_wide), bf16(n_deep, n_wide)],
            table,
            *near_rows,
            near_stack,
            far_stack,
            flops=6 * n_tall * n_deep * n_wide,
        )
        held = rounds(far_part, min(TIE2, reach), reach, held)
        arrived = lax.ppermute(held[0], both, streams[0])
        arrived, near_side = lax.optimization_barrier((arrived, near_side))
        far_rows = [arrived + held[1]]
        far_rows += [swap(x, 1) for x in far_rows]
        scale_inv = float((samples.shape[0] * n_rows) ** -0.5)
        half, wide, n_way = n_tall // 4, n_wide // 2, n_feat // 2
        whole = lambda a: pl.BlockSpec(a.shape, lambda i, t: (0, 0))
        tiled = lambda a: pl.BlockSpec((a.shape[0] // 2, a.shape[1]), lambda i, t: (i, 0))
        half_a, half_b = f32(2 * half, n_high // 2 * wide), f32(half, n_high * wide)
        squares, rows_split = [bf16(n_tall, n_deep)] * 2, [bf16(n_deep, f_wide)] * 2
        *sent, sq_high, sq_low, far_high, far_low = call(
            functools.partial(sent_kernel, scale_inv, n_high, len(far_rows)),
            [half_a] * 2 + [half_b] * 2 + squares + rows_split,
            table,
            *near_side,
            *far_rows,
            grid=(2,),
            in_specs=[tiled(x) for x in near_side[:3]] + [whole(x) for x in near_side[3:]] + [whole(x) for x in far_rows],
            out_specs=[tiled(half_a)] * 2
            + [whole(half_b)] * 2
            + [tiled(x) for x in squares]
            + [whole(x) for x in rows_split],
            flops=6 * n_tall * n_deep * (f_wide + n_wide // 2 * n_high),
        )
        kept = call(
            functools.partial(kept_kernel, scale_inv, n_high),
            [half_a] * 2 + [half_b] * 2,
            table,
            sq_high,
            sq_low,
            *near_side[3:],
            far_high,
            far_low,
            grid=(2,),
            in_specs=[tiled(x) for x in squares] + [whole(x) for x in near_side[3:]] + [whole(x) for x in rows_split],
            out_specs=[tiled(half_a)] * 2 + [whole(half_b)] * 2,
            flops=6 * n_tall * n_deep * (n_wide // 2 * n_high),
        )

        def over_rows(x, bits):
            for bit in bits:
                cols = x.shape[1] // 2
                x = x[:, :cols] + swap(x[:, cols:], bit)
            return x

        def over_chips(a_sent, b_sent, a_kept, b_kept):
            a = over_rows(a_kept + swap(a_sent, high_bits[-1]), high_bits[-2::-1])
            a = a[:half] + swap_feat(a[half:], 1)
            b = over_rows(b_kept + swap_feat(b_sent, 1), high_bits[::-1])
            joint = jnp.concatenate([a, b], axis=1)
            step = half // n_way
            parts = [joint[k * step : (k + 1) * step] for k in range(n_way)]
            return parts[:1] + [swap_feat(part, 2 * k) for k, part in enumerate(parts) if k]

        parts = over_chips(*sent[::2], *kept[::2]) + over_chips(*sent[1::2], *kept[1::2])
        height = 2 * half // n_way
        kept, sent = call(functools.partial(divide_kernel, core_at), [f32(height, wide)] * 2, table, *parts)
        return call(
            functools.partial(assemble_kernel, core_at), [f32(wide, 2 * height)], table, kept, swap(sent, 1)
        )[0]

    placed = (P("rows", "feat"), P("feat", "rows"), P("rows", "feat"))
    return jax.shard_map(
        on_device, mesh=mesh, in_specs=placed, out_specs=P("rows", "feat"), check_vma=False
    )
```
